32 devices in a mesh: grp: 4 (over z), dev: 8 (over y, x, core).
Axes of the slice: x: 2, y: 2, z: 4, core: 2. Of those that a mesh axis runs over, the one named last changes fastest.
Arguments:
- adjoint_load: float32 [1024, 64, 128], P(('grp', 'dev')), as said below
- local_ops: float32 [4, 2016, 64, 64], P(None, ('grp', 'dev')), as said below
- coarse_ops: float32 [4, 4, 7, 64, 64], P(None, 'grp'), as said below
- slab_order: int32 [32, 32], P(('grp', 'dev')), may hold values from 0 to 31, each once within a row
Outputs:
- slab_adjoint: float32 [1024, 64, 128], P(('grp', 'dev'))
The draws below stay inside these ranges and needn't reach their ends.
Inputs may be any that keep to these rules, and one draw needn't show every extreme that they name: `local_ops`: blocks of kind 3 approximate the inverses of the diagonal blocks. `coarse_ops`: same four kinds of blocks as local_ops. `adjoint_load`: real-valued right-hand sides. `slab_order`: each row lists every one of the 32 rows of one device once.
All inputs are finite; a program needn't handle non-finite values.
Results may differ from the reference program's by a relative error of at most 0.0001.
Values sent between devices are 32-bit elements; how exact they have to be, the bound alone decides.
A program may use at most 64 MiB of HBM per device.

```python
import math
import jax
import jax.numpy as jnp
from jax import lax

B = 64
K = 128
R0 = 32
AGG = 3
GROUPS = 4
GROUP_ROWS = 256
FINE_ROWS = 1024
OPS_ROWS = 2016
CROWS = 7


def make_blocks(key, leading):
    keys = jax.random.split(key, 6)
    shape = leading + (B, B)
    identity = (lax.broadcasted_iota(jnp.int32, (B, B), 0) == lax.broadcasted_iota(jnp.int32, (B, B), 1)).astype(jnp.float32)
    noise = 0.03 * jax.random.normal(keys[0], shape, jnp.float32)
    dscale = jnp.exp(jax.random.uniform(keys[1], leading + (1, 1), jnp.float32, math.log(2.0), math.log(5.0)))
    lower_frac = jax.random.uniform(keys[2], leading + (1, 1), jnp.float32, 0.4, 0.48)
    upper_frac = jax.random.uniform(keys[3], leading + (1, 1), jnp.float32, 0.4, 0.48)
    lower_noise = 0.02 * jax.random.normal(keys[4], shape, jnp.float32)
    upper_noise = 0.02 * jax.random.normal(keys[5], shape, jnp.float32)
    lower = -dscale * lower_frac * (identity + lower_noise)
    upper = -dscale * upper_frac * (identity + upper_noise)
    diagonal = dscale * (identity + noise)
    inverse = (identity - noise) / dscale
    return jnp.stack([lower, diagonal, upper, inverse])


def draw_local_ops(key, part):
    return make_blocks(key, (OPS_ROWS,))


def draw_coarse_ops(key, part):
    return make_blocks(jax.random.fold_in(key, 7), (GROUPS, CROWS))


def draw_adjoint_load(key, part):
    base = jax.random.normal(key, (FINE_ROWS, B, K), jnp.float32)
    return base + 0.5


def setup_inputs(seed: int = 0) -> dict:
    arg_keys = jax.random.split(jax.random.key(seed), 5)
    return {
        "adjoint_load": draw_adjoint_load(jax.random.fold_in(arg_keys[4], 71), 0),
        "local_ops": draw_local_ops(jax.random.fold_in(arg_keys[4], 71), 0),
        "coarse_ops": draw_coarse_ops(jax.random.fold_in(arg_keys[4], 71), 0),
        "slab_order": jax.vmap(lambda own: jax.random.permutation(own, R0))(jax.random.split(arg_keys[3], (FINE_ROWS // R0))).reshape((FINE_ROWS // R0, R0)).astype(jnp.int32),
    }


damping = 0.8


def block_apply(blocks, values):
    return jnp.einsum("rij,rjk->rik", blocks, values, precision=lax.Precision.HIGHEST)


def operate(blocks, values):
    border = jnp.zeros((1,) + values.shape[1:], values.dtype)
    before = jnp.concatenate([border, values[:-1]], axis=0)
    following = jnp.concatenate([values[1:], border], axis=0)
    return (block_apply(blocks[0], before) + block_apply(blocks[1], values)) + block_apply(blocks[2], following)


def halve_rows(residual):
    paired = residual.reshape((residual.shape[0] // 2, 2) + residual.shape[1:])
    return 0.5 * (paired[:, 0] + paired[:, 1])


def vcycle(levels, section_id, source):
    blocks = levels[section_id]
    solution = damping * block_apply(blocks[3], source)
    if section_id + 1 < len(levels):
        residual = source - operate(blocks, solution)
        correction = vcycle(levels, section_id + 1, halve_rows(residual))
        solution = solution + jnp.repeat(correction, 2, axis=0)
    solution = solution + damping * block_apply(blocks[3], source - operate(blocks, solution))
    return solution


def reference(adjoint_load, local_ops, coarse_ops, slab_order):
    local_levels = R0.bit_length()
    devices = GROUP_ROWS // R0
    per_device = 2 * R0 - 1
    results = []
    for group_id in range(GROUPS):
        blocks_all = local_ops[:, group_id * devices * per_device:(group_id + 1) * devices * per_device]
        blocks_all = blocks_all.reshape(4, devices, per_device, B, B)
        levels = []
        offset = 0
        for level_id in range(local_levels):
            height = R0 >> level_id
            shaped = blocks_all[:, :, offset:offset + height]
            levels.append(shaped.reshape(4, devices * height, B, B))
            offset += height
        for section_id in range(1, AGG + 1):
            begin_row = devices - devices // 2 ** (section_id - 1)
            levels.append(coarse_ops[:, group_id, begin_row:begin_row + devices // 2 ** section_id])
        source = adjoint_load[group_id * GROUP_ROWS:(group_id + 1) * GROUP_ROWS]
        initial = vcycle(levels, 0, source)
        residual = source - operate(levels[0], initial)
        results.append(initial + vcycle(levels, 0, residual))
    stacked = jnp.stack(results).reshape(GROUPS, devices, R0, B, K)
    ordering = slab_order.reshape(GROUPS, devices, R0)
    permuted = jax.vmap(jax.vmap(lambda values, picks: values[picks]))(stacked, ordering)
    pieces = permuted.reshape(GROUPS, devices, GROUPS, R0 // GROUPS, B, K)
    return jnp.transpose(pieces, (2, 1, 0, 3, 4, 5)).reshape(FINE_ROWS, B, K)
```

```python
import functools
import jax
import jax.numpy as jnp
from jax import lax
from jax.experimental import pallas as pl
from jax.experimental.pallas import tpu as pltpu
from jax.sharding import PartitionSpec as P

damping = 0.8
GROUP = 4
CHUNKS = 4
f32 = jnp.float32
bf16 = jnp.bfloat16


def split(value):
    high = value.astype(bf16)
    return high, (value - high.astype(f32)).astype(bf16)


def over_rows(low, high, body, group=GROUP):
    full = (high - low) // group
    if full > 1:
        def step(index, carry):
            body([low + index * group + t for t in range(group)])
            return carry
        lax.fori_loop(0, full, step, 0)
        low += full * group
    while low < high:
        body(list(range(low, min(low + group, high))))
        low += group


def kernel(
    plan,
    load, ops, coarse, order,
    out,
    raw, raw_s, raw_a, raw_g, raw_c,
    a_hi, a_lo, s3, b, x, e, x_hi, x_lo, f_hi, f_lo, staged,
    local_sem, b_send, b_recv, o_send, o_recv, go_send, go_recv, g_send, g_recv, t_send, t_recv,
):
    devices, groups, heights, bases, wide, wide_bases = plan
    levels = len(heights)
    rows = heights[0]
    per_slab = rows // groups
    dev = lax.axis_index("dev")
    grp = lax.axis_index("grp")
    has = (dev > 0, dev < devices - 1)
    offsets = [2 * rows - 2 * rows // 2**l for l in range(levels + 1)]
    gather_base = wide_bases[0]

    local = []

    def fetch(src, dst):
        copy = pltpu.make_async_copy(src, dst, local_sem.at[len(local)])
        copy.start()
        local.append(copy)
        return copy

    load_copy = fetch(load, b.at[0, pl.ds(bases[0] + 2, rows)])
    piece = rows // CHUNKS
    fine_copies = [
        fetch(ops.at[:, pl.ds(c * piece, piece)], raw.at[:, pl.ds(c * piece, piece)])
        for c in range(CHUNKS)
    ]
    rest = ops.shape[1] - rows
    rest_copy = fetch(ops.at[:, pl.ds(rows, rest)], raw.at[:, pl.ds(rows, rest)])
    coarse_copy = fetch(coarse, raw_c)

    barrier = pltpu.get_barrier_semaphore()
    for k in range(1, devices):
        pl.semaphore_signal(barrier, inc=1, device_id={"dev": lax.rem(dev + k, devices)},
                            device_id_type=pl.DeviceIdType.MESH)
    for k in range(1, groups):
        pl.semaphore_signal(barrier, inc=1, device_id={"grp": lax.rem(grp + k, groups)},
                            device_id_type=pl.DeviceIdType.MESH)
    pl.semaphore_wait(barrier, devices - 1 + groups - 1)

    def remote(src, dst, send, recv, axis, target):
        return pltpu.make_async_remote_copy(
            src_ref=src, dst_ref=dst, send_sem=send, recv_sem=recv,
            device_id={axis: target}, device_id_type=pl.DeviceIdType.MESH)

    def b_halo(cycle, l, side):
        n, base = heights[l], bases[l]
        start = n - 2 if side == 0 else 0
        if cycle == 0 and l == 0:
            src = load.at[pl.ds(start, 2)]
        else:
            src = b.at[cycle, pl.ds(base + 2 + start, 2)]
        dst = b.at[cycle, pl.ds(base + (0 if side == 0 else n + 2), 2)]
        target = dev + 1 if side == 0 else dev - 1
        return remote(src, dst, b_send.at[cycle, l, side], b_recv.at[cycle, l, side], "dev", target)

    def o_halo(l, side, part):
        n = heights[l]
        if part == 0:
            start = n - 2 if side == 0 else 0
            src, dst = ops.at[pl.ds(3, 1), pl.ds(offsets[l] + start, 2)], raw_s.at[l, side]
        else:
            start = n - 1 if side == 0 else 0
            src, dst = ops.at[pl.ds(0, 3), pl.ds(offsets[l] + start, 1)], raw_a.at[l, side]
        target = dev + 1 if side == 0 else dev - 1
        return remote(src, dst, o_send.at[l, side, part], o_recv.at[l, side, part], "dev", target)

    def on_send(side, act):
        pl.when(has[1 - side])(act)

    def send_b(cycle, l):
        for side in range(2):
            on_send(side, lambda side=side: b_halo(cycle, l, side).start())

    def go_copy(k, sender, target):
        return remote(ops.at[:, pl.ds(offsets[levels], 1)], raw_g.at[sender],
                      go_send.at[k], go_recv.at[sender], "dev", target)

    def g_copy(cycle, k, sender, target):
        row = b.at[cycle, pl.ds(gather_base + 2 + sender, 1)]
        return remote(row, row, g_send.at[cycle, k], g_recv.at[cycle, sender], "dev", target)

    send_b(0, 0)
    for l in range(levels):
        for side in range(2):
            def begin(side=side, l=l):
                o_halo(l, side, 0).start()
                o_halo(l, side, 1).start()
            on_send(side, begin)
    for k in range(1, devices):
        go_copy(k, dev, lax.rem(dev + k, devices)).start()

    def pack_s(row, block):
        hi, lo = split(damping * block)
        hi, lo = hi.astype(f32), lo.astype(f32)
        s3[row] = jnp.concatenate([hi, hi, lo], axis=1).astype(bf16)

    def pack_a(row, lower, middle, upper):
        hi, lo = split(jnp.concatenate([lower, middle, upper], axis=1))
        a_hi[row] = hi
        a_lo[row] = lo

    def pack_own(l, low, high):
        def body(js):
            for j in js:
                source = offsets[l] + j
                row = bases[l] + 2 + j
                pack_a(row, raw[0, source], raw[1, source], raw[2, source])
                pack_s(row, raw[3, source])
        over_rows(low, high, body, 2)

    def s_mul(row, value):
        hi, lo = split(value)
        return jnp.dot(s3[row], jnp.concatenate([hi, lo, hi], axis=0), preferred_element_type=f32)

    def a_mul(row, j, hi_ref, lo_ref):
        hi = hi_ref[pl.ds(j - 1, 3)].reshape(-1, hi_ref.shape[-1])
        lo = lo_ref[pl.ds(j - 1, 3)].reshape(-1, lo_ref.shape[-1])
        high = a_hi[row]
        return (jnp.dot(high, lo, preferred_element_type=f32)
                + jnp.dot(a_lo[row], hi, preferred_element_type=f32)
                + jnp.dot(high, hi, preferred_element_type=f32))

    def presmooth(cycle, base, low, high):
        def body(js):
            values = [s_mul(base + j, b[cycle, base + j]) for j in js]
            halves = [split(v) for v in values]
            for j, v, (hi, lo) in zip(js, values, halves):
                x[base + j] = v
                x_hi[j] = hi
                x_lo[j] = lo
        over_rows(low, high, body)

    def restrict(cycle, base, pairs, store):
        def body(ps):
            js = [j for p in ps for j in (2 + 2 * p, 3 + 2 * p)]
            r = [b[cycle, base + j] - a_mul(base + j, j, x_hi, x_lo) for j in js]
            for t, p in enumerate(ps):
                store(p, 0.5 * (r[2 * t] + r[2 * t + 1]))
        for low, high in pairs:
            over_rows(low, high, body, 2)

    def correct(base, low, high, e_row):
        def body(ps):
            vs = []
            for p in ps:
                add = e[e_row(p + 1)]
                vs += [x[base + 2 * p] + add, x[base + 2 * p + 1] + add]
            halves = [split(v) for v in vs]
            js = [j for p in ps for j in (2 * p, 2 * p + 1)]
            for j, v, (hi, lo) in zip(js, vs, halves):
                x[base + j] = v
                x_hi[j] = hi
                x_lo[j] = lo
        over_rows(low // 2, high // 2, body, 2)

    def smoothed(cycle, base, js):
        r = [b[cycle, base + j] - a_mul(base + j, j, x_hi, x_lo) for j in js]
        return [x[base + j] + s_mul(base + j, v) for j, v in zip(js, r)]

    def postsmooth(cycle, base, low, high, keep=False):
        def body(js):
            values = smoothed(cycle, base, js)
            for j, v in zip(js, values):
                e[base + j] = v
            if keep:
                for j, v in zip(js, values):
                    f_hi[j], f_lo[j] = split(v)
        over_rows(low, high, body)

    def zero_rows(ref, indices):
        for i in indices:
            ref[i] = jnp.zeros(ref.shape[1:], ref.dtype)

    def down_local(cycle, l):
        n, base = heights[l], bases[l]
        if cycle == 0:
            if l == 0:
                load_copy.wait()
                for c in range(CHUNKS):
                    fine_copies[c].wait()
                    pack_own(0, c * piece, (c + 1) * piece)
            else:
                if l == 1:
                    rest_copy.wait()
                pack_own(l, 0, n)
        presmooth(cycle, base, 2, n + 2)
        for side in range(2):
            outer = (0, 1) if side == 0 else (n + 2, n + 3)
            inner = 1 if side == 0 else n + 2

            def arrive(side=side, outer=outer, inner=inner):
                b_halo(cycle, l, side).wait_recv()
                if cycle == 0:
                    o_halo(l, side, 0).wait_recv()
                    o_halo(l, side, 1).wait_recv()
                    for t, j in enumerate(outer):
                        pack_s(base + j, raw_s[l, side, 0, t])
                    pack_a(base + inner, raw_a[l, side, 0, 0], raw_a[l, side, 1, 0], raw_a[l, side, 2, 0])

            pl.when(has[side])(arrive)
            if cycle == 0:
                def blank(outer=outer, inner=inner):
                    for j in outer:
                        s3[base + j] = jnp.zeros(s3.shape[1:], bf16)
                        b[0, base + j] = jnp.zeros(b.shape[2:], f32)
                        b[1, base + j] = jnp.zeros(b.shape[2:], f32)
                    a_hi[base + inner] = jnp.zeros(a_hi.shape[1:], bf16)
                    a_lo[base + inner] = jnp.zeros(a_lo.shape[1:], bf16)
                pl.when(jnp.logical_not(has[side]))(blank)
        js = [0, 1, n + 2, n + 3]
        values = [s_mul(base + j, b[cycle, base + j]) for j in js]
        for j, v in zip(js, values):
            x[base + j] = v
            x_hi[j], x_lo[j] = split(v)
        half = n // 2
        if l + 1 < levels:
            def store(p, c):
                b[cycle, bases[l + 1] + 2 + p] = c
            if half > 4:
                restrict(cycle, base, [(0, 2), (half - 2, half)], store)
                send_b(cycle, l + 1)
                restrict(cycle, base, [(2, half - 2)], store)
            else:
                restrict(cycle, base, [(0, half)], store)
                send_b(cycle, l + 1)
        else:
            def store(p, c):
                b[cycle, gather_base + 2 + dev] = c
            restrict(cycle, base, [(0, half)], store)
            for k in range(1, devices):
                g_copy(cycle, k, dev, lax.rem(dev + k, devices)).start()

    def solve_wide(cycle):
        if cycle == 0:
            own = offsets[levels]
            pack_a(gather_base + 2 + dev, raw[0, own], raw[1, own], raw[2, own])
            pack_s(gather_base + 2 + dev, raw[3, own])
            coarse_copy.wait()
            first = 0
            for m in range(1, len(wide)):
                def body(js, first=first, m=m):
                    for j in js:
                        row = wide_bases[m] + 2 + j
                        pack_a(row, raw_c[0, 0, first + j], raw_c[1, 0, first + j], raw_c[2, 0, first + j])
                        pack_s(row, raw_c[3, 0, first + j])
                over_rows(0, wide[m], body, 2)
                first += wide[m]

            def take(k, carry):
                sender = lax.rem(dev + k, devices)
                go_copy(0, sender, sender).wait_recv()
                row = gather_base + 2 + sender
                pack_a(row, raw_g[sender, 0, 0], raw_g[sender, 1, 0], raw_g[sender, 2, 0])
                pack_s(row, raw_g[sender, 3, 0])
                return carry
            lax.fori_loop(1, devices, take, 0)
            zero_rows(e, [gather_base + 1, gather_base + wide[0] + 2])
        for k in range(1, devices):
            sender = lax.rem(dev + k, devices)
            g_copy(cycle, 0, sender, sender).wait_recv()

        def visit(m):
            n, base = wide[m], wide_bases[m]
            pads = [1, n + 2]
            presmooth(cycle, base, 2, n + 2)
            if m + 1 < len(wide):
                zero_rows(x_hi, pads)
                zero_rows(x_lo, pads)

                def store(p, c):
                    b[cycle, wide_bases[m + 1] + 2 + p] = c
                restrict(cycle, base, [(0, n // 2)], store)
                visit(m + 1)
                correct(base, 2, n + 2, lambda i: wide_bases[m + 1] + i)
            zero_rows(x_hi, pads)
            zero_rows(x_lo, pads)
            postsmooth(cycle, base, 2, n + 2)
        visit(0)

    def up_to(cycle, l):
        if l == levels - 1:
            correct(bases[l], 0, heights[l] + 4, lambda i: gather_base + dev + i)
        else:
            correct(bases[l], 0, heights[l] + 4, lambda i: bases[l + 1] + i)

    for l in range(levels):
        down_local(0, l)
    solve_wide(0)
    for l in reversed(range(levels)):
        up_to(0, l)
        postsmooth(0, bases[l], 1, heights[l] + 3, keep=l == 0)

    base = bases[0]

    def again(js):
        values = [b[0, base + j] - a_mul(base + j, j, f_hi, f_lo) for j in js]
        for j, v in zip(js, values):
            b[1, base + j] = v
    again([2, 3, rows, rows + 1])
    send_b(1, 0)
    over_rows(4, rows, again)

    for l in range(levels):
        down_local(1, l)
    solve_wide(1)
    for l in reversed(range(1, levels)):
        up_to(1, l)
        postsmooth(1, bases[l], 1, heights[l] + 3)
    up_to(1, 0)

    def slab_copy(k, slab, sender):
        return remote(staged.at[pl.ds(slab * per_slab, per_slab)], out.at[pl.ds(sender * per_slab, per_slab)],
                      t_send.at[k], t_recv.at[sender], "grp", slab)

    steps = [(k + groups // 2) % groups for k in range(groups)]
    steps = [k for k in steps if k] + [0]
    for k in steps:
        slab = lax.rem(grp + k, groups)

        def body(us, slab=slab):
            ts = [slab * per_slab + u for u in us]
            js = [order[0, t] + 2 for t in ts]
            values = smoothed(1, base, js)
            values = [v + e[base + j] for v, j in zip(values, js)]
            for t, v in zip(ts, values):
                staged[t] = v
        over_rows(0, per_slab, body)
        if k:
            slab_copy(k, slab, grp).start()
        else:
            own = pltpu.make_async_copy(staged.at[pl.ds(slab * per_slab, per_slab)],
                                        out.at[pl.ds(grp * per_slab, per_slab)], local_sem.at[0])
            own.start()
            own.wait()

    for l in range(levels):
        for side in range(2):
            def left(l=l, side=side):
                b_halo(0, l, side).wait_send()
                b_halo(1, l, side).wait_send()
                o_halo(l, side, 0).wait_send()
                o_halo(l, side, 1).wait_send()
            on_send(side, left)
    for k in range(1, devices):
        target = lax.rem(dev + k, devices)
        go_copy(k, dev, target).wait_send()
        g_copy(0, k, dev, target).wait_send()
        g_copy(1, k, dev, target).wait_send()
    for k in range(1, groups):
        slab = lax.rem(grp + k, groups)
        slab_copy(k, slab, grp).wait_send()
        slab_copy(k, slab, slab).wait_recv()


def shards(adjoint_load, local_ops, coarse_ops, slab_order):
    rows, size, cases = adjoint_load.shape
    devices = lax.axis_size("dev")
    groups = lax.axis_size("grp")
    levels = rows.bit_length() - 1
    heights = [rows >> l for l in range(levels)]
    wide = [devices]
    while sum(wide[1:]) < coarse_ops.shape[2]:
        wide.append(wide[-1] // 2)
    bases, total = [], 0
    for n in heights + wide:
        bases.append(total)
        total += n + 4
    plan = (devices, groups, heights, bases[:levels], wide, bases[levels:])
    most = max(rows, devices) + 4
    kinds = local_ops.shape[0]
    dma = pltpu.SemaphoreType.DMA
    scratch = [
        pltpu.VMEM(local_ops.shape, f32),
        pltpu.VMEM((levels, 2, 1, 2, size, size), f32),
        pltpu.VMEM((levels, 2, 3, 1, size, size), f32),
        pltpu.VMEM((devices, kinds, 1, size, size), f32),
        pltpu.VMEM(coarse_ops.shape, f32),
        pltpu.VMEM((total, size, 3 * size), bf16),
        pltpu.VMEM((total, size, 3 * size), bf16),
        pltpu.VMEM((total, size, 3 * size), bf16),
        pltpu.VMEM((2, total, size, cases), f32),
        pltpu.VMEM((total, size, cases), f32),
        pltpu.VMEM((total, size, cases), f32),
        pltpu.VMEM((most, size, cases), bf16),
        pltpu.VMEM((most, size, cases), bf16),
        pltpu.VMEM((rows + 4, size, cases), bf16),
        pltpu.VMEM((rows + 4, size, cases), bf16),
        pltpu.VMEM((rows, size, cases), f32),
        dma((CHUNKS + 3,)),
        dma((2, levels, 2)), dma((2, levels, 2)),
        dma((levels, 2, 2)), dma((levels, 2, 2)),
        dma((devices,)), dma((devices,)),
        dma((2, devices)), dma((2, devices)),
        dma((groups,)), dma((groups,)),
    ]
    anywhere = pl.BlockSpec(memory_space=pl.ANY)
    return pl.pallas_call(
        functools.partial(kernel, plan),
        out_shape=jax.ShapeDtypeStruct(adjoint_load.shape, f32),
        in_specs=[anywhere, anywhere, anywhere, pl.BlockSpec(memory_space=pltpu.SMEM)],
        out_specs=anywhere,
        scratch_shapes=scratch,
        compiler_params=pltpu.CompilerParams(
            collective_id=0, has_side_effects=True, vmem_limit_bytes=62 * 2**20),
    )(adjoint_load, local_ops, coarse_ops, slab_order)


def solution(mesh):
    placed = (
        P(("grp", "dev"), None, None),
        P(None, ("grp", "dev"), None, None),
        P(None, "grp", None, None, None),
        P(("grp", "dev"), None),
    )
    return jax.shard_map(
        shards, mesh=mesh, in_specs=placed, out_specs=P(("grp", "dev"), None, None), check_vma=False
    )
```

```python
import functools
import jax
import jax.numpy as jnp
from jax import lax
from jax.experimental import pallas as pl
from jax.experimental.pallas import tpu as pltpu
from jax.sharding import PartitionSpec as P

damping = 0.8
GROUP = 4
CHUNKS = 4
f32 = jnp.float32
bf16 = jnp.bfloat16


def split(value):
    high = value.astype(bf16)
    return high, (value - high.astype(f32)).astype(bf16)


def over_rows(low, high, body, group=GROUP):
    full = (high - low) // group
    if full > 1:
        def step(index, carry):
            body([low + index * group + t for t in range(group)])
            return carry
        lax.fori_loop(0, full, step, 0)
        low += full * group
    while low < high:
        body(list(range(low, min(low + group, high))))
        low += group


def kernel(
    plan,
    load, ops, coarse, order,
    out,
    raw, raw_s, raw_a, raw_g, raw_c,
    a_op, r_op, s4, b, x, first, x_two, f_two, staged,
    local_sem, b_send, b_recv, o_send, o_recv, go_send, go_recv, g_send, g_recv, t_send, t_recv,
):
    devices, groups, heights, bases, wide, wide_bases = plan
    levels = len(heights)
    rows = heights[0]
    per_slab = rows // groups
    dev = lax.axis_index("dev")
    grp = lax.axis_index("grp")
    has = (dev > 0, dev < devices - 1)
    offsets = [2 * rows - 2 * rows // 2**l for l in range(levels + 1)]
    gather_base = wide_bases[0]

    local = []

    def fetch(src, dst):
        copy = pltpu.make_async_copy(src, dst, local_sem.at[len(local)])
        copy.start()
        local.append(copy)
        return copy

    load_copy = fetch(load, b.at[0, pl.ds(bases[0] + 2, rows)])
    piece = rows // CHUNKS
    fine_copies = [
        fetch(ops.at[:, pl.ds(c * piece, piece)], raw.at[:, pl.ds(c * piece, piece)])
        for c in range(CHUNKS)
    ]
    rest = ops.shape[1] - rows
    rest_copy = fetch(ops.at[:, pl.ds(rows, rest)], raw.at[:, pl.ds(rows, rest)])
    coarse_copy = fetch(coarse, raw_c)

    barrier = pltpu.get_barrier_semaphore()
    for k in range(1, devices):
        pl.semaphore_signal(barrier, inc=1, device_id={"dev": lax.rem(dev + k, devices)},
                            device_id_type=pl.DeviceIdType.MESH)
    for k in range(1, groups):
        pl.semaphore_signal(barrier, inc=1, device_id={"grp": lax.rem(grp + k, groups)},
                            device_id_type=pl.DeviceIdType.MESH)
    pl.semaphore_wait(barrier, devices - 1 + groups - 1)

    def remote(src, dst, send, recv, axis, target):
        return pltpu.make_async_remote_copy(
            src_ref=src, dst_ref=dst, send_sem=send, recv_sem=recv,
            device_id={axis: target}, device_id_type=pl.DeviceIdType.MESH)

    def b_halo(cycle, l, side):
        n, base = heights[l], bases[l]
        start = n - 2 if side == 0 else 0
        if cycle == 0 and l == 0:
            src = load.at[pl.ds(start, 2)]
        else:
            src = b.at[cycle, pl.ds(base + 2 + start, 2)]
        dst = b.at[cycle, pl.ds(base + (0 if side == 0 else n + 2), 2)]
        target = dev + 1 if side == 0 else dev - 1
        return remote(src, dst, b_send.at[cycle, l, side], b_recv.at[cycle, l, side], "dev", target)

    def o_halo(l, side, part):
        n = heights[l]
        if part == 0:
            start = n - 2 if side == 0 else 0
            src, dst = ops.at[pl.ds(3, 1), pl.ds(offsets[l] + start, 2)], raw_s.at[l, side]
        else:
            start = n - 1 if side == 0 else 0
            src, dst = ops.at[pl.ds(0, 3), pl.ds(offsets[l] + start, 1)], raw_a.at[l, side]
        target = dev + 1 if side == 0 else dev - 1
        return remote(src, dst, o_send.at[l, side, part], o_recv.at[l, side, part], "dev", target)

    def on_send(side, act):
        pl.when(has[1 - side])(act)

    def send_b(cycle, l):
        for side in range(2):
            on_send(side, lambda side=side: b_halo(cycle, l, side).start())

    def go_copy(k, sender, target):
        return remote(ops.at[:, pl.ds(offsets[levels], 1)], raw_g.at[sender],
                      go_send.at[k], go_recv.at[sender], "dev", target)

    def g_copy(cycle, k, sender, target):
        row = b.at[cycle, pl.ds(gather_base + 2 + sender, 1)]
        return remote(row, row, g_send.at[cycle, k], g_recv.at[cycle, sender], "dev", target)

    send_b(0, 0)
    for l in range(levels):
        for side in range(2):
            def begin(side=side, l=l):
                o_halo(l, side, 0).start()
                o_halo(l, side, 1).start()
            on_send(side, begin)
    for k in range(1, devices):
        go_copy(k, dev, lax.rem(dev + k, devices)).start()

    size = x.shape[1]
    cases = x.shape[2]

    def pack_s(row, block):
        hi, lo = split(damping * block)
        hi, lo = hi.astype(f32), lo.astype(f32)
        s4[row] = jnp.concatenate([hi, hi, lo, lo], axis=1).astype(bf16)

    def placed_a(odd, lower, middle, upper):
        none = jnp.zeros_like(middle)
        blocks = [none, lower, middle, upper] if odd else [lower, middle, upper, none]
        return jnp.concatenate(blocks, axis=1)

    def put(ref, row, value):
        hi, lo = split(value)
        ref[row, pl.ds(0, size)] = hi
        ref[row, pl.ds(size, size)] = lo

    def pack_pair(base, p, blocks):
        row = base + 2 + 2 * p
        (l0, m0, u0, inv0), (l1, m1, u1, inv1) = blocks
        even, odd = placed_a(False, l0, m0, u0), placed_a(True, l1, m1, u1)
        put(a_op, row, even)
        put(a_op, row + 1, odd)
        put(r_op, base // 2 + 1 + p, 0.5 * (even + odd))
        pack_s(row, inv0)
        pack_s(row + 1, inv1)

    def pack_own(l, low, high):
        def body(ps):
            for p in ps:
                source = offsets[l] + 2 * p
                pack_pair(bases[l], p, [[raw[k, source + t] for k in range(4)] for t in range(2)])
        over_rows(low // 2, high // 2, body, 2)

    def s_mul(row, value):
        hi, lo = split(value)
        return jnp.dot(s4[row], jnp.concatenate([hi, lo, hi, lo], axis=0), preferred_element_type=f32)

    def gathered(product):
        upper, lower = product[:size], product[size:]
        return (lower[:, cases:] + (upper[:, cases:] + lower[:, :cases])) + upper[:, :cases]

    def window(ref, low):
        return ref[pl.ds(low, 4)].reshape(4 * size, 2 * cases)

    def a_pair(base, j, ref):
        both = a_op[pl.ds(base + j, 2)].reshape(4 * size, 4 * size)
        product = jnp.dot(both, window(ref, j - 1), preferred_element_type=f32)
        return [gathered(product[: 2 * size]), gathered(product[2 * size :])]

    def a_single(base, j, low, ref):
        return gathered(jnp.dot(a_op[base + j], window(ref, low), preferred_element_type=f32))

    def two(ref, j, value):
        hi, lo = split(value)
        ref[j, :, pl.ds(0, cases)] = hi
        ref[j, :, pl.ds(cases, cases)] = lo

    def presmooth(cycle, base, low, high):
        def body(js):
            values = [s_mul(base + j, b[cycle, base + j]) for j in js]
            for j, v in zip(js, values):
                x[base + j] = v
                two(x_two, j, v)
        over_rows(low, high, body, 8)

    def restrict(cycle, base, pairs, store):
        def body(ps):
            values = []
            for p in ps:
                j = 2 + 2 * p
                product = jnp.dot(r_op[base // 2 + 1 + p], window(x_two, j - 1), preferred_element_type=f32)
                values.append(0.5 * (b[cycle, base + j] + b[cycle, base + j + 1]) - gathered(product))
            for p, v in zip(ps, values):
                store(p, v)
        for low, high in pairs:
            over_rows(low, high, body, 4)

    def correct(base, low, high, e_row):
        def body(ps):
            js, vs = [], []
            for p in ps:
                add = x[e_row(p + 1)]
                js += [2 * p, 2 * p + 1]
                vs += [x[base + 2 * p] + add, x[base + 2 * p + 1] + add]
            for j, v in zip(js, vs):
                x[base + j] = v
                two(x_two, j, v)
        over_rows(low // 2, high // 2, body, 2)

    def finish(cycle, base, js, products):
        r = [b[cycle, base + j] - v for j, v in zip(js, products)]
        return [x[base + j] + s_mul(base + j, v) for j, v in zip(js, r)]

    def settle(base, js, values, keep):
        for j, v in zip(js, values):
            if keep:
                first[j] = v
                two(f_two, j, v)
            else:
                x[base + j] = v

    def postsmooth(cycle, base, n, halo, keep=False):
        def body(ps):
            js, products = [], []
            for p in ps:
                js += [2 + 2 * p, 3 + 2 * p]
                products += a_pair(base, 2 + 2 * p, x_two)
            settle(base, js, finish(cycle, base, js, products), keep)
        if n > 1:
            over_rows(0, n // 2, body, 2)
        if halo:
            js = [1, n + 2]
            products = [a_single(base, 1, 0, x_two), a_single(base, n + 2, n, x_two)]
            settle(base, js, finish(cycle, base, js, products), keep)
        if n == 1:
            settle(base, [2], finish(cycle, base, [2], [a_single(base, 2, 1, x_two)]), keep)

    def zero_rows(ref, indices):
        for i in indices:
            ref[i] = jnp.zeros(ref.shape[1:], ref.dtype)

    def down_local(cycle, l):
        n, base = heights[l], bases[l]
        if cycle == 0:
            if l == 0:
                load_copy.wait()
                for c in range(CHUNKS):
                    fine_copies[c].wait()
                    pack_own(0, c * piece, (c + 1) * piece)
            else:
                if l == 1:
                    rest_copy.wait()
                pack_own(l, 0, n)
        presmooth(cycle, base, 2, n + 2)
        for side in range(2):
            outer = (0, 1) if side == 0 else (n + 2, n + 3)

            def arrive(side=side, outer=outer):
                b_halo(cycle, l, side).wait_recv()
                if cycle == 0:
                    o_halo(l, side, 0).wait_recv()
                    for t, j in enumerate(outer):
                        pack_s(base + j, raw_s[l, side, 0, t])

            pl.when(has[side])(arrive)
            if cycle == 0:
                def blank(outer=outer):
                    for j in outer:
                        s4[base + j] = jnp.zeros(s4.shape[1:], bf16)
                        b[0, base + j] = jnp.zeros(b.shape[2:], f32)
                        b[1, base + j] = jnp.zeros(b.shape[2:], f32)
                pl.when(jnp.logical_not(has[side]))(blank)
        js = [0, 1, n + 2, n + 3]
        values = [s_mul(base + j, b[cycle, base + j]) for j in js]
        for j, v in zip(js, values):
            x[base + j] = v
            two(x_two, j, v)
        half = n // 2
        if l + 1 < levels:
            def store(p, c):
                b[cycle, bases[l + 1] + 2 + p] = c
            if half > 4:
                restrict(cycle, base, [(0, 2), (half - 2, half)], store)
                send_b(cycle, l + 1)
                restrict(cycle, base, [(2, half - 2)], store)
            else:
                restrict(cycle, base, [(0, half)], store)
                send_b(cycle, l + 1)
        else:
            def store(p, c):
                b[cycle, gather_base + 2 + dev] = c
            restrict(cycle, base, [(0, half)], store)
            for k in range(1, devices):
                g_copy(cycle, k, dev, lax.rem(dev + k, devices)).start()

    def solve_wide(cycle):
        if cycle == 0:
            own = offsets[levels]
            raw_g[dev] = raw[:, pl.ds(own, 1)]
            coarse_copy.wait()
            start = 0
            for m in range(1, len(wide)):
                def body(ps, start=start, m=m):
                    for p in ps:
                        pack_pair(wide_bases[m], p, [
                            [raw_c[k, 0, start + 2 * p + t] for k in range(4)] for t in range(2)])
                if wide[m] > 1:
                    over_rows(0, wide[m] // 2, body, 2)
                else:
                    row = wide_bases[m] + 2
                    put(a_op, row, placed_a(False, *[raw_c[k, 0, start] for k in range(3)]))
                    pack_s(row, raw_c[3, 0, start])
                start += wide[m]
            for k in range(1, devices):
                sender = lax.rem(dev + k, devices)
                go_copy(0, sender, sender).wait_recv()

            def body(ps):
                for p in ps:
                    pack_pair(gather_base, p, [[raw_g[2 * p + t, k, 0] for k in range(4)] for t in range(2)])
            over_rows(0, devices // 2, body, 2)
            zero_rows(x, [gather_base + 1, gather_base + wide[0] + 2])
        for k in range(1, devices):
            sender = lax.rem(dev + k, devices)
            g_copy(cycle, 0, sender, sender).wait_recv()

        def visit(m):
            n, base = wide[m], wide_bases[m]
            pads = [1, n + 2] + ([n + 3] if n == 1 else [])
            presmooth(cycle, base, 2, n + 2)
            if m + 1 < len(wide):
                zero_rows(x_two, pads)

                def store(p, c):
                    b[cycle, wide_bases[m + 1] + 2 + p] = c
                restrict(cycle, base, [(0, n // 2)], store)
                visit(m + 1)
                correct(base, 2, n + 2, lambda i: wide_bases[m + 1] + i)
            zero_rows(x_two, pads)
            postsmooth(cycle, base, n, False)
        visit(0)

    def up_to(cycle, l):
        n, base = heights[l], bases[l]
        if l == levels - 1:
            correct(base, 0, n + 4, lambda i: gather_base + dev + i)
        else:
            correct(base, 0, n + 4, lambda i: bases[l + 1] + i)
        if cycle == 0:
            for side in range(2):
                row = base + (1 if side == 0 else n + 2)

                def arrive(side=side, row=row):
                    o_halo(l, side, 1).wait_recv()
                    put(a_op, row, placed_a(side == 1, *[raw_a[l, side, k, 0] for k in range(3)]))

                def blank(row=row):
                    a_op[row] = jnp.zeros(a_op.shape[1:], bf16)
                pl.when(has[side])(arrive)
                pl.when(jnp.logical_not(has[side]))(blank)

    for l in range(levels):
        down_local(0, l)
    solve_wide(0)
    for l in reversed(range(levels)):
        up_to(0, l)
        postsmooth(0, bases[l], heights[l], True, keep=l == 0)

    base = bases[0]

    def again(ps):
        js, products = [], []
        for p in ps:
            js += [2 + 2 * p, 3 + 2 * p]
            products += a_pair(base, 2 + 2 * p, f_two)
        values = [b[0, base + j] - v for j, v in zip(js, products)]
        for j, v in zip(js, values):
            b[1, base + j] = v
    again([0, rows // 2 - 1])
    send_b(1, 0)
    over_rows(1, rows // 2 - 1, again, 2)

    for l in range(levels):
        down_local(1, l)
    solve_wide(1)
    for l in reversed(range(1, levels)):
        up_to(1, l)
        postsmooth(1, bases[l], heights[l], True)
    up_to(1, 0)

    def slab_copy(k, slab, sender):
        return remote(staged.at[pl.ds(slab * per_slab, per_slab)], out.at[pl.ds(sender * per_slab, per_slab)],
                      t_send.at[k], t_recv.at[sender], "grp", slab)

    sent = []
    for k in [k for k in range(groups) if k != groups // 2] + [groups // 2]:
        slab = lax.rem(grp + groups // 2 + 2 * (k // 2), groups)
        if k % 2:
            slab = slab + 1 - 2 * lax.rem(slab, 2)

        def body(us, slab=slab):
            ts = [slab * per_slab + u for u in us]
            js = [order[0, t] + 2 for t in ts]
            products = []
            for j in js:
                low = j - 1 - lax.rem(j, 2)
                products.append(a_single(base, j, low, x_two))
            values = finish(1, base, js, products)
            values = [v + first[j] for v, j in zip(values, js)]
            for t, v in zip(ts, values):
                staged[t] = v
        own = k == groups // 2
        over_rows(0, per_slab, body)
        if own:
            keep = pltpu.make_async_copy(staged.at[pl.ds(slab * per_slab, per_slab)],
                                         out.at[pl.ds(grp * per_slab, per_slab)], local_sem.at[0])
            keep.start()
        else:
            slab_copy(k, slab, grp).start()
            sent.append((k, slab))
    keep.wait()

    for l in range(levels):
        for side in range(2):
            def left(l=l, side=side):
                b_halo(0, l, side).wait_send()
                b_halo(1, l, side).wait_send()
                o_halo(l, side, 0).wait_send()
                o_halo(l, side, 1).wait_send()
            on_send(side, left)
    for k in range(1, devices):
        target = lax.rem(dev + k, devices)
        go_copy(k, dev, target).wait_send()
        g_copy(0, k, dev, target).wait_send()
        g_copy(1, k, dev, target).wait_send()
    for k, slab in sent:
        slab_copy(k, slab, grp).wait_send()
        slab_copy(k, slab, slab).wait_recv()


def shards(adjoint_load, local_ops, coarse_ops, slab_order):
    rows, size, cases = adjoint_load.shape
    devices = lax.axis_size("dev")
    groups = lax.axis_size("grp")
    levels = rows.bit_length() - 1
    heights = [rows >> l for l in range(levels)]
    wide = [devices]
    while sum(wide[1:]) < coarse_ops.shape[2]:
        wide.append(wide[-1] // 2)
    bases, total = [], 0
    for n in heights + wide:
        bases.append(total)
        total += n + 4
    plan = (devices, groups, heights, bases[:levels], wide, bases[levels:])
    most = max(rows, devices) + 4
    kinds = local_ops.shape[0]
    dma = pltpu.SemaphoreType.DMA
    scratch = [
        pltpu.VMEM(local_ops.shape, f32),
        pltpu.VMEM((levels, 2, 1, 2, size, size), f32),
        pltpu.VMEM((levels, 2, 3, 1, size, size), f32),
        pltpu.VMEM((devices, kinds, 1, size, size), f32),
        pltpu.VMEM(coarse_ops.shape, f32),
        pltpu.VMEM((total, 2 * size, 4 * size), bf16),
        pltpu.VMEM((total // 2 + 1, 2 * size, 4 * size), bf16),
        pltpu.VMEM((total, size, 4 * size), bf16),
        pltpu.VMEM((2, total, size, cases), f32),
        pltpu.VMEM((total, size, cases), f32),
        pltpu.VMEM((rows + 4, size, cases), f32),
        pltpu.VMEM((most, size, 2 * cases), bf16),
        pltpu.VMEM((rows + 4, size, 2 * cases), bf16),
        pltpu.VMEM((rows, size, cases), f32),
        dma((CHUNKS + 3,)),
        dma((2, levels, 2)), dma((2, levels, 2)),
        dma((levels, 2, 2)), dma((levels, 2, 2)),
        dma((devices,)), dma((devices,)),
        dma((2, devices)), dma((2, devices)),
        dma((groups,)), dma((groups,)),
    ]
    anywhere = pl.BlockSpec(memory_space=pl.ANY)
    return pl.pallas_call(
        functools.partial(kernel, plan),
        out_shape=jax.ShapeDtypeStruct(adjoint_load.shape, f32),
        in_specs=[anywhere, anywhere, anywhere, pl.BlockSpec(memory_space=pltpu.SMEM)],
        out_specs=anywhere,
        scratch_shapes=scratch,
        compiler_params=pltpu.CompilerParams(
            collective_id=0, has_side_effects=True, vmem_limit_bytes=62 * 2**20),
    )(adjoint_load, local_ops, coarse_ops, slab_order)


def solution(mesh):
    placed = (
        P(("grp", "dev"), None, None),
        P(None, ("grp", "dev"), None, None),
        P(None, "grp", None, None, None),
        P(("grp", "dev"), None),
    )
    return jax.shard_map(
        shards, mesh=mesh, in_specs=placed, out_specs=P(("grp", "dev"), None, None), check_vma=False
    )
```

```python
import functools
import jax
import jax.numpy as jnp
from jax import lax
from jax.experimental import pallas as pl
from jax.experimental.pallas import tpu as pltpu
from jax.sharding import PartitionSpec as P

damping = 0.8
GROUP = 4
CHUNKS = 4
f32 = jnp.float32
bf16 = jnp.bfloat16


def split(value):
    high = value.astype(bf16)
    return high, (value - high.astype(f32)).astype(bf16)


def over_rows(low, high, body, group=GROUP):
    full = (high - low) // group
    if full > 1:
        def step(index, carry):
            body([low + index * group + t for t in range(group)])
            return carry
        lax.fori_loop(0, full, step, 0)
        low += full * group
    while low < high:
        body(list(range(low, min(low + group, high))))
        low += group


def kernel(
    plan,
    load, ops, coarse, order,
    out,
    raw, raw_s, raw_a, raw_g, raw_c,
    a_op, r_op, s4, b, x, first, x_two, f_two, staged,
    local_sem, b_send, b_recv, o_send, o_recv, go_send, go_recv, g_send, g_recv, t_send, t_recv,
):
    devices, groups, heights, bases, wide, wide_bases = plan
    levels = len(heights)
    rows = heights[0]
    per_slab = rows // groups
    dev = lax.axis_index("dev")
    grp = lax.axis_index("grp")
    has = (dev > 0, dev < devices - 1)
    offsets = [2 * rows - 2 * rows // 2**l for l in range(levels + 1)]
    gather_base = wide_bases[0]

    local = []

    def fetch(src, dst):
        copy = pltpu.make_async_copy(src, dst, local_sem.at[len(local)])
        copy.start()
        local.append(copy)
        return copy

    load_copy = fetch(load, b.at[0, pl.ds(bases[0] + 2, rows)])
    piece = rows // CHUNKS
    fine_copies = [
        fetch(ops.at[:, pl.ds(c * piece, piece)], raw.at[:, pl.ds(c * piece, piece)])
        for c in range(CHUNKS)
    ]
    rest = ops.shape[1] - rows
    rest_copy = fetch(ops.at[:, pl.ds(rows, rest)], raw.at[:, pl.ds(rows, rest)])
    coarse_copy = fetch(coarse, raw_c)

    barrier = pltpu.get_barrier_semaphore()
    for k in range(1, devices):
        pl.semaphore_signal(barrier, inc=1, device_id={"dev": lax.rem(dev + k, devices)},
                            device_id_type=pl.DeviceIdType.MESH)
    for k in range(1, groups):
        pl.semaphore_signal(barrier, inc=1, device_id={"grp": lax.rem(grp + k, groups)},
                            device_id_type=pl.DeviceIdType.MESH)
    pl.semaphore_wait(barrier, devices - 1 + groups - 1)

    def remote(src, dst, send, recv, axis, target):
        return pltpu.make_async_remote_copy(
            src_ref=src, dst_ref=dst, send_sem=send, recv_sem=recv,
            device_id={axis: target}, device_id_type=pl.DeviceIdType.MESH)

    def b_halo(cycle, l, side):
        n, base = heights[l], bases[l]
        start = n - 2 if side == 0 else 0
        if cycle == 0 and l == 0:
            src = load.at[pl.ds(start, 2)]
        else:
            src = b.at[cycle, pl.ds(base + 2 + start, 2)]
        dst = b.at[cycle, pl.ds(base + (0 if side == 0 else n + 2), 2)]
        target = dev + 1 if side == 0 else dev - 1
        return remote(src, dst, b_send.at[cycle, l, side], b_recv.at[cycle, l, side], "dev", target)

    def o_halo(l, side, part):
        n = heights[l]
        if part == 0:
            start = n - 2 if side == 0 else 0
            src, dst = ops.at[pl.ds(3, 1), pl.ds(offsets[l] + start, 2)], raw_s.at[l, side]
        else:
            start = n - 1 if side == 0 else 0
            src, dst = ops.at[pl.ds(0, 3), pl.ds(offsets[l] + start, 1)], raw_a.at[l, side]
        target = dev + 1 if side == 0 else dev - 1
        return remote(src, dst, o_send.at[l, side, part], o_recv.at[l, side, part], "dev", target)

    def on_send(side, act):
        pl.when(has[1 - side])(act)

    def send_b(cycle, l):
        for side in range(2):
            on_send(side, lambda side=side: b_halo(cycle, l, side).start())

    def go_copy(k, sender, target):
        return remote(ops.at[:, pl.ds(offsets[levels], 1)], raw_g.at[sender],
                      go_send.at[k], go_recv.at[sender], "dev", target)

    def g_copy(cycle, k, sender, target):
        row = b.at[cycle, pl.ds(gather_base + 2 + sender, 1)]
        return remote(row, row, g_send.at[cycle, k], g_recv.at[cycle, sender], "dev", target)

    send_b(0, 0)
    for l in range(levels):
        for side in range(2):
            def begin(side=side, l=l):
                o_halo(l, side, 0).start()
                o_halo(l, side, 1).start()
            on_send(side, begin)
    for k in range(1, devices):
        go_copy(k, dev, lax.rem(dev + k, devices)).start()

    size = x.shape[1]
    cases = x.shape[2]

    def pack_s(row, block):
        hi, lo = split(damping * block)
        hi, lo = hi.astype(f32), lo.astype(f32)
        s4[row] = jnp.concatenate([hi, hi, lo, lo], axis=1).astype(bf16)

    def placed_a(odd, lower, middle, upper):
        none = jnp.zeros_like(middle)
        blocks = [none, lower, middle, upper] if odd else [lower, middle, upper, none]
        return jnp.concatenate(blocks, axis=1)

    def put(ref, row, value):
        hi, lo = split(value)
        ref[row, pl.ds(0, size)] = hi
        ref[row, pl.ds(size, size)] = lo

    def pack_pair(base, p, blocks):
        row = base + 2 + 2 * p
        (l0, m0, u0, inv0), (l1, m1, u1, inv1) = blocks
        even, odd = placed_a(False, l0, m0, u0), placed_a(True, l1, m1, u1)
        put(a_op, row, even)
        put(a_op, row + 1, odd)
        put(r_op, base // 2 + 1 + p, 0.5 * (even + odd))
        pack_s(row, inv0)
        pack_s(row + 1, inv1)

    def pack_own(l, low, high):
        def body(ps):
            for p in ps:
                source = offsets[l] + 2 * p
                pack_pair(bases[l], p, [[raw[k, source + t] for k in range(4)] for t in range(2)])
        over_rows(low // 2, high // 2, body, 2)

    def s_mul(row, value):
        hi, lo = split(value)
        return jnp.dot(s4[row], jnp.concatenate([hi, lo, hi, lo], axis=0), preferred_element_type=f32)

    def gathered(product):
        upper, lower = product[:size], product[size:]
        return (lower[:, cases:] + (upper[:, cases:] + lower[:, :cases])) + upper[:, :cases]

    def window(ref, low):
        return ref[pl.ds(low, 4)].reshape(4 * size, 2 * cases)

    def a_pair(base, j, ref):
        both = a_op[pl.ds(base + j, 2)].reshape(4 * size, 4 * size)
        product = jnp.dot(both, window(ref, j - 1), preferred_element_type=f32)
        return [gathered(product[: 2 * size]), gathered(product[2 * size :])]

    def a_single(base, j, low, ref):
        return gathered(jnp.dot(a_op[base + j], window(ref, low), preferred_element_type=f32))

    def two(ref, j, value):
        hi, lo = split(value)
        ref[j, :, pl.ds(0, cases)] = hi
        ref[j, :, pl.ds(cases, cases)] = lo

    def presmooth(cycle, base, low, high):
        def body(js):
            values = [s_mul(base + j, b[cycle, base + j]) for j in js]
            for j, v in zip(js, values):
                x[base + j] = v
                two(x_two, j, v)
        over_rows(low, high, body, 16)

    def restrict(cycle, base, pairs, store):
        def body(ps):
            values = []
            for p in ps:
                j = 2 + 2 * p
                product = jnp.dot(r_op[base // 2 + 1 + p], window(x_two, j - 1), preferred_element_type=f32)
                values.append(0.5 * (b[cycle, base + j] + b[cycle, base + j + 1]) - gathered(product))
            for p, v in zip(ps, values):
                store(p, v)
        if isinstance(pairs, list):
            body(pairs)
        else:
            over_rows(*pairs, body, 6)

    def correct(base, low, high, e_row):
        def body(ps):
            js, vs = [], []
            for p in ps:
                add = x[e_row(p + 1)]
                js += [2 * p, 2 * p + 1]
                vs += [x[base + 2 * p] + add, x[base + 2 * p + 1] + add]
            for j, v in zip(js, vs):
                x[base + j] = v
                two(x_two, j, v)
        over_rows(low // 2, high // 2, body, 6)

    def finish(cycle, base, js, products):
        r = [b[cycle, base + j] - v for j, v in zip(js, products)]
        return [x[base + j] + s_mul(base + j, v) for j, v in zip(js, r)]

    def settle(base, js, values, keep):
        for j, v in zip(js, values):
            if keep:
                first[j] = v
                two(f_two, j, v)
            else:
                x[base + j] = v

    def postsmooth(cycle, base, n, halo, keep=False):
        def body(ps, singles=()):
            js, products = [], []
            for p in ps:
                js += [2 + 2 * p, 3 + 2 * p]
                products += a_pair(base, 2 + 2 * p, x_two)
            for j, low in singles:
                js.append(j)
                products.append(a_single(base, j, low, x_two))
            settle(base, js, finish(cycle, base, js, products), keep)
        if n == 1:
            body([], [(2, 1)])
            return
        head = max(0, (n // 2 - 1) // 4 * 4)
        over_rows(0, head, body, 4)
        body(list(range(head, n // 2)), [(1, 0), (n + 2, n)] if halo else [])

    def zero_rows(ref, indices):
        for i in indices:
            ref[i] = jnp.zeros(ref.shape[1:], ref.dtype)

    def down_local(cycle, l):
        n, base = heights[l], bases[l]
        if cycle == 0:
            if l == 0:
                load_copy.wait()
                for c in range(CHUNKS):
                    fine_copies[c].wait()
                    pack_own(0, c * piece, (c + 1) * piece)
            else:
                if l == 1:
                    rest_copy.wait()
                pack_own(l, 0, n)
        presmooth(cycle, base, 2, n + 2)
        for side in range(2):
            outer = (0, 1) if side == 0 else (n + 2, n + 3)

            def arrive(side=side, outer=outer):
                b_halo(cycle, l, side).wait_recv()
                if cycle == 0:
                    o_halo(l, side, 0).wait_recv()
                    for t, j in enumerate(outer):
                        pack_s(base + j, raw_s[l, side, 0, t])

            pl.when(has[side])(arrive)
            if cycle == 0:
                def blank(outer=outer):
                    for j in outer:
                        s4[base + j] = jnp.zeros(s4.shape[1:], bf16)
                        b[0, base + j] = jnp.zeros(b.shape[2:], f32)
                        b[1, base + j] = jnp.zeros(b.shape[2:], f32)
                pl.when(jnp.logical_not(has[side]))(blank)
        js = [0, 1, n + 2, n + 3]
        values = [s_mul(base + j, b[cycle, base + j]) for j in js]
        for j, v in zip(js, values):
            x[base + j] = v
            two(x_two, j, v)
        half = n // 2
        if l + 1 < levels:
            def store(p, c):
                b[cycle, bases[l + 1] + 2 + p] = c
            if half > 4:
                restrict(cycle, base, [0, 1, half - 2, half - 1], store)
                send_b(cycle, l + 1)
                restrict(cycle, base, (2, half - 2), store)
            else:
                restrict(cycle, base, (0, half), store)
                send_b(cycle, l + 1)
        else:
            def store(p, c):
                b[cycle, gather_base + 2 + dev] = c
            restrict(cycle, base, (0, half), store)
            for k in range(1, devices):
                g_copy(cycle, k, dev, lax.rem(dev + k, devices)).start()

    def solve_wide(cycle):
        if cycle == 0:
            own = offsets[levels]
            raw_g[dev] = raw[:, pl.ds(own, 1)]
            coarse_copy.wait()
            start = 0
            for m in range(1, len(wide)):
                def body(ps, start=start, m=m):
                    for p in ps:
                        pack_pair(wide_bases[m], p, [
                            [raw_c[k, 0, start + 2 * p + t] for k in range(4)] for t in range(2)])
                if wide[m] > 1:
                    over_rows(0, wide[m] // 2, body, 2)
                else:
                    row = wide_bases[m] + 2
                    put(a_op, row, placed_a(False, *[raw_c[k, 0, start] for k in range(3)]))
                    pack_s(row, raw_c[3, 0, start])
                start += wide[m]
            for k in range(1, devices):
                sender = lax.rem(dev + k, devices)
                go_copy(0, sender, sender).wait_recv()

            def body(ps):
                for p in ps:
                    pack_pair(gather_base, p, [[raw_g[2 * p + t, k, 0] for k in range(4)] for t in range(2)])
            over_rows(0, devices // 2, body, 2)
            zero_rows(x, [gather_base + 1, gather_base + wide[0] + 2])
        for k in range(1, devices):
            sender = lax.rem(dev + k, devices)
            g_copy(cycle, 0, sender, sender).wait_recv()

        def visit(m):
            n, base = wide[m], wide_bases[m]
            pads = [1, n + 2] + ([n + 3] if n == 1 else [])
            presmooth(cycle, base, 2, n + 2)
            if m + 1 < len(wide):
                zero_rows(x_two, pads)

                def store(p, c):
                    b[cycle, wide_bases[m + 1] + 2 + p] = c
                restrict(cycle, base, (0, n // 2), store)
                visit(m + 1)
                correct(base, 2, n + 2, lambda i: wide_bases[m + 1] + i)
            zero_rows(x_two, pads)
            postsmooth(cycle, base, n, False)
        visit(0)

    def up_to(cycle, l):
        n, base = heights[l], bases[l]
        if l == levels - 1:
            correct(base, 0, n + 4, lambda i: gather_base + dev + i)
        else:
            correct(base, 0, n + 4, lambda i: bases[l + 1] + i)
        if cycle == 0:
            for side in range(2):
                row = base + (1 if side == 0 else n + 2)

                def arrive(side=side, row=row):
                    o_halo(l, side, 1).wait_recv()
                    put(a_op, row, placed_a(side == 1, *[raw_a[l, side, k, 0] for k in range(3)]))

                def blank(row=row):
                    a_op[row] = jnp.zeros(a_op.shape[1:], bf16)
                pl.when(has[side])(arrive)
                pl.when(jnp.logical_not(has[side]))(blank)

    for l in range(levels):
        down_local(0, l)
    solve_wide(0)
    for l in reversed(range(levels)):
        up_to(0, l)
        postsmooth(0, bases[l], heights[l], True, keep=l == 0)

    base = bases[0]

    def again(ps):
        js, products = [], []
        for p in ps:
            js += [2 + 2 * p, 3 + 2 * p]
            products += a_pair(base, 2 + 2 * p, f_two)
        values = [b[0, base + j] - v for j, v in zip(js, products)]
        for j, v in zip(js, values):
            b[1, base + j] = v
    again([0, rows // 2 - 1])
    send_b(1, 0)
    over_rows(1, rows // 2 - 1, again, 4)

    for l in range(levels):
        down_local(1, l)
    solve_wide(1)
    for l in reversed(range(1, levels)):
        up_to(1, l)
        postsmooth(1, bases[l], heights[l], True)
    up_to(1, 0)

    def slab_copy(k, slab, sender):
        return remote(staged.at[pl.ds(slab * per_slab, per_slab)], out.at[pl.ds(sender * per_slab, per_slab)],
                      t_send.at[k], t_recv.at[sender], "grp", slab)

    sent = []
    for k in [k for k in range(groups) if k != groups // 2] + [groups // 2]:
        slab = lax.rem(grp + groups // 2 + 2 * (k // 2), groups)
        if k % 2:
            slab = slab + 1 - 2 * lax.rem(slab, 2)

        def body(us, slab=slab):
            ts = [slab * per_slab + u for u in us]
            js = [order[0, t] + 2 for t in ts]
            products = []
            for j in js:
                low = j - 1 - lax.rem(j, 2)
                products.append(a_single(base, j, low, x_two))
            values = finish(1, base, js, products)
            values = [v + first[j] for v, j in zip(values, js)]
            for t, v in zip(ts, values):
                staged[t] = v
        own = k == groups // 2
        over_rows(0, per_slab, body, 8)
        if own:
            keep = pltpu.make_async_copy(staged.at[pl.ds(slab * per_slab, per_slab)],
                                         out.at[pl.ds(grp * per_slab, per_slab)], local_sem.at[0])
            keep.start()
        else:
            slab_copy(k, slab, grp).start()
            sent.append((k, slab))
    keep.wait()

    for l in range(levels):
        for side in range(2):
            def left(l=l, side=side):
                b_halo(0, l, side).wait_send()
                b_halo(1, l, side).wait_send()
                o_halo(l, side, 0).wait_send()
                o_halo(l, side, 1).wait_send()
            on_send(side, left)
    for k in range(1, devices):
        target = lax.rem(dev + k, devices)
        go_copy(k, dev, target).wait_send()
        g_copy(0, k, dev, target).wait_send()
        g_copy(1, k, dev, target).wait_send()
    for k, slab in sent:
        slab_copy(k, slab, grp).wait_send()
        slab_copy(k, slab, slab).wait_recv()


def shards(adjoint_load, local_ops, coarse_ops, slab_order):
    rows, size, cases = adjoint_load.shape
    devices = lax.axis_size("dev")
    groups = lax.axis_size("grp")
    levels = rows.bit_length() - 1
    heights = [rows >> l for l in range(levels)]
    wide = [devices]
    while sum(wide[1:]) < coarse_ops.shape[2]:
        wide.append(wide[-1] // 2)
    bases, total = [], 0
    for n in heights + wide:
        bases.append(total)
        total += n + 4
    plan = (devices, groups, heights, bases[:levels], wide, bases[levels:])
    most = max(rows, devices) + 4
    kinds = local_ops.shape[0]
    dma = pltpu.SemaphoreType.DMA
    scratch = [
        pltpu.VMEM(local_ops.shape, f32),
        pltpu.VMEM((levels, 2, 1, 2, size, size), f32),
        pltpu.VMEM((levels, 2, 3, 1, size, size), f32),
        pltpu.VMEM((devices, kinds, 1, size, size), f32),
        pltpu.VMEM(coarse_ops.shape, f32),
        pltpu.VMEM((total, 2 * size, 4 * size), bf16),
        pltpu.VMEM((total // 2 + 1, 2 * size, 4 * size), bf16),
        pltpu.VMEM((total, size, 4 * size), bf16),
        pltpu.VMEM((2, total, size, cases), f32),
        pltpu.VMEM((total, size, cases), f32),
        pltpu.VMEM((rows + 4, size, cases), f32),
        pltpu.VMEM((most, size, 2 * cases), bf16),
        pltpu.VMEM((rows + 4, size, 2 * cases), bf16),
        pltpu.VMEM((rows, size, cases), f32),
        dma((CHUNKS + 3,)),
        dma((2, levels, 2)), dma((2, levels, 2)),
        dma((levels, 2, 2)), dma((levels, 2, 2)),
        dma((devices,)), dma((devices,)),
        dma((2, devices)), dma((2, devices)),
        dma((groups,)), dma((groups,)),
    ]
    anywhere = pl.BlockSpec(memory_space=pl.ANY)
    return pl.pallas_call(
        functools.partial(kernel, plan),
        out_shape=jax.ShapeDtypeStruct(adjoint_load.shape, f32),
        in_specs=[anywhere, anywhere, anywhere, pl.BlockSpec(memory_space=pltpu.SMEM)],
        out_specs=anywhere,
        scratch_shapes=scratch,
        compiler_params=pltpu.CompilerParams(
            collective_id=0, has_side_effects=True, vmem_limit_bytes=62 * 2**20),
    )(adjoint_load, local_ops, coarse_ops, slab_order)


def solution(mesh):
    placed = (
        P(("grp", "dev"), None, None),
        P(None, ("grp", "dev"), None, None),
        P(None, "grp", None, None, None),
        P(("grp", "dev"), None),
    )
    return jax.shard_map(
        shards, mesh=mesh, in_specs=placed, out_specs=P(("grp", "dev"), None, None), check_vma=False
    )
```

```python
import functools
import jax
import jax.numpy as jnp
from jax import lax
from jax.experimental import pallas as pl
from jax.experimental.pallas import tpu as pltpu
from jax.sharding import PartitionSpec as P

damping = 0.8
GROUP = 4
CHUNKS = 4
f32 = jnp.float32
bf16 = jnp.bfloat16


def split(value):
    high = value.astype(bf16)
    return high, (value - high.astype(f32)).astype(bf16)


def over_rows(low, high, body, group=GROUP):
    full = (high - low) // group
    if full > 1:
        def step(index, carry):
            body([low + index * group + t for t in range(group)])
            return carry
        lax.fori_loop(0, full, step, 0)
        low += full * group
    while low < high:
        body(list(range(low, min(low + group, high))))
        low += group


def kernel(
    plan,
    load, ops, coarse, order,
    out,
    raw, raw_s, raw_a, raw_g, raw_c,
    a_op, r_op, s4, b, x, first, x_two, f_two, staged,
    local_sem, b_send, b_recv, o_send, o_recv, go_send, go_recv, g_send, g_recv, t_send, t_recv,
):
    devices, groups, heights, bases, wide, wide_bases = plan
    levels = len(heights)
    rows = heights[0]
    per_slab = rows // groups
    dev = lax.axis_index("dev")
    grp = lax.axis_index("grp")
    has = (dev > 0, dev < devices - 1)
    offsets = [2 * rows - 2 * rows // 2**l for l in range(levels + 1)]
    gather_base = wide_bases[0]

    local = []

    def fetch(src, dst):
        copy = pltpu.make_async_copy(src, dst, local_sem.at[len(local)])
        copy.start()
        local.append(copy)
        return copy

    load_copy = fetch(load, b.at[0, pl.ds(bases[0] + 2, rows)])
    piece = rows // CHUNKS
    fine_copies = [
        fetch(ops.at[:, pl.ds(c * piece, piece)], raw.at[:, pl.ds(c * piece, piece)])
        for c in range(CHUNKS)
    ]
    rest = ops.shape[1] - rows
    rest_copy = fetch(ops.at[:, pl.ds(rows, rest)], raw.at[:, pl.ds(rows, rest)])
    coarse_copy = fetch(coarse, raw_c)

    barrier = pltpu.get_barrier_semaphore()
    for k in range(1, devices):
        pl.semaphore_signal(barrier, inc=1, device_id={"dev": lax.rem(dev + k, devices)},
                            device_id_type=pl.DeviceIdType.MESH)
    for k in range(1, groups):
        pl.semaphore_signal(barrier, inc=1, device_id={"grp": lax.rem(grp + k, groups)},
                            device_id_type=pl.DeviceIdType.MESH)
    pl.semaphore_wait(barrier, devices - 1 + groups - 1)

    def remote(src, dst, send, recv, axis, target):
        return pltpu.make_async_remote_copy(
            src_ref=src, dst_ref=dst, send_sem=send, recv_sem=recv,
            device_id={axis: target}, device_id_type=pl.DeviceIdType.MESH)

    def b_halo(cycle, l, side):
        n, base = heights[l], bases[l]
        start = n - 2 if side == 0 else 0
        if cycle == 0 and l == 0:
            src = load.at[pl.ds(start, 2)]
        else:
            src = b.at[cycle, pl.ds(base + 2 + start, 2)]
        dst = b.at[cycle, pl.ds(base + (0 if side == 0 else n + 2), 2)]
        target = dev + 1 if side == 0 else dev - 1
        return remote(src, dst, b_send.at[cycle, l, side], b_recv.at[cycle, l, side], "dev", target)

    def o_halo(l, side, part):
        n = heights[l]
        if part == 0:
            start = n - 2 if side == 0 else 0
            src, dst = ops.at[pl.ds(3, 1), pl.ds(offsets[l] + start, 2)], raw_s.at[l, side]
        else:
            start = n - 1 if side == 0 else 0
            src, dst = ops.at[pl.ds(0, 3), pl.ds(offsets[l] + start, 1)], raw_a.at[l, side]
        target = dev + 1 if side == 0 else dev - 1
        return remote(src, dst, o_send.at[l, side, part], o_recv.at[l, side, part], "dev", target)

    def on_send(side, act):
        pl.when(has[1 - side])(act)

    def send_b(cycle, l):
        for side in range(2):
            on_send(side, lambda side=side: b_halo(cycle, l, side).start())

    def go_copy(k, sender, target):
        return remote(ops.at[:, pl.ds(offsets[levels], 1)], raw_g.at[sender],
                      go_send.at[k], go_recv.at[sender], "dev", target)

    def g_copy(cycle, k, sender, target):
        row = b.at[cycle, pl.ds(gather_base + 2 + sender, 1)]
        return remote(row, row, g_send.at[cycle, k], g_recv.at[cycle, sender], "dev", target)

    send_b(0, 0)
    def send_o(part, these):
        for l in these:
            for side in range(2):
                on_send(side, lambda l=l, side=side: o_halo(l, side, part).start())

    send_o(0, [0])

    size = x.shape[1]
    cases = x.shape[2]

    def pack_s(row, block):
        hi, lo = split(damping * block)
        hi, lo = hi.astype(f32), lo.astype(f32)
        s4[row] = jnp.concatenate([hi, hi, lo, lo], axis=1).astype(bf16)

    def placed_a(odd, lower, middle, upper):
        none = jnp.zeros_like(middle)
        blocks = [none, lower, middle, upper] if odd else [lower, middle, upper, none]
        return jnp.concatenate(blocks, axis=1)

    def put(ref, row, value):
        hi, lo = split(value)
        ref[row, pl.ds(0, size)] = hi
        ref[row, pl.ds(size, size)] = lo

    def pack_pair(base, p, blocks):
        row = base + 2 + 2 * p
        (l0, m0, u0, inv0), (l1, m1, u1, inv1) = blocks
        even, odd = placed_a(False, l0, m0, u0), placed_a(True, l1, m1, u1)
        put(a_op, row, even)
        put(a_op, row + 1, odd)
        put(r_op, base // 2 + 1 + p, 0.5 * (even + odd))
        pack_s(row, inv0)
        pack_s(row + 1, inv1)

    def pack_own(l, low, high):
        def body(ps):
            for p in ps:
                source = offsets[l] + 2 * p
                pack_pair(bases[l], p, [[raw[k, source + t] for k in range(4)] for t in range(2)])
        over_rows(low // 2, high // 2, body, 2)

    def s_mul(row, value):
        hi, lo = split(value)
        return jnp.dot(s4[row], jnp.concatenate([hi, lo, hi, lo], axis=0), preferred_element_type=f32)

    def gathered(product):
        upper, lower = product[:size], product[size:]
        return (lower[:, cases:] + (upper[:, cases:] + lower[:, :cases])) + upper[:, :cases]

    def window(ref, low):
        return ref[pl.ds(low, 4)].reshape(4 * size, 2 * cases)

    def a_pair(base, j, ref):
        both = a_op[pl.ds(base + j, 2)].reshape(4 * size, 4 * size)
        product = jnp.dot(both, window(ref, j - 1), preferred_element_type=f32)
        return [gathered(product[: 2 * size]), gathered(product[2 * size :])]

    def a_single(base, j, low, ref):
        return gathered(jnp.dot(a_op[base + j], window(ref, low), preferred_element_type=f32))

    def two(ref, j, value):
        hi, lo = split(value)
        ref[j, :, pl.ds(0, cases)] = hi
        ref[j, :, pl.ds(cases, cases)] = lo

    def presmooth(cycle, base, low, high):
        def body(js):
            values = [s_mul(base + j, b[cycle, base + j]) for j in js]
            for j, v in zip(js, values):
                x[base + j] = v
                two(x_two, j, v)
        over_rows(low, high, body, 16)

    def restrict(cycle, base, pairs, store):
        def body(ps):
            values = []
            for p in ps:
                j = 2 + 2 * p
                product = jnp.dot(r_op[base // 2 + 1 + p], window(x_two, j - 1), preferred_element_type=f32)
                values.append(0.5 * (b[cycle, base + j] + b[cycle, base + j + 1]) - gathered(product))
            for p, v in zip(ps, values):
                store(p, v)
        if isinstance(pairs, list):
            body(pairs)
        else:
            over_rows(*pairs, body, 6)

    def correct(base, low, high, e_row):
        def body(ps):
            js, vs = [], []
            for p in ps:
                add = x[e_row(p + 1)]
                js += [2 * p, 2 * p + 1]
                vs += [x[base + 2 * p] + add, x[base + 2 * p + 1] + add]
            for j, v in zip(js, vs):
                x[base + j] = v
                two(x_two, j, v)
        over_rows(low // 2, high // 2, body, 6)

    def finish(cycle, base, js, products):
        r = [b[cycle, base + j] - v for j, v in zip(js, products)]
        return [x[base + j] + s_mul(base + j, v) for j, v in zip(js, r)]

    def settle(base, js, values, keep):
        for j, v in zip(js, values):
            if keep:
                first[j] = v
                two(f_two, j, v)
            else:
                x[base + j] = v

    def postsmooth(cycle, base, n, halo, keep=False):
        def body(ps, singles=()):
            js, products = [], []
            for p in ps:
                js += [2 + 2 * p, 3 + 2 * p]
                products += a_pair(base, 2 + 2 * p, x_two)
            for j, low in singles:
                js.append(j)
                products.append(a_single(base, j, low, x_two))
            settle(base, js, finish(cycle, base, js, products), keep)
        if n == 1:
            body([], [(2, 1)])
            return
        head = max(0, (n // 2 - 1) // 4 * 4)
        over_rows(0, head, body, 4)
        body(list(range(head, n // 2)), [(1, 0), (n + 2, n)] if halo else [])

    def zero_rows(ref, indices):
        for i in indices:
            ref[i] = jnp.zeros(ref.shape[1:], ref.dtype)

    def down_local(cycle, l):
        n, base = heights[l], bases[l]
        if cycle == 0:
            if l == 0:
                load_copy.wait()
                for c in range(CHUNKS):
                    fine_copies[c].wait()
                    pack_own(0, c * piece, (c + 1) * piece)
                    if c == 0:
                        send_o(0, range(1, levels))
            else:
                if l == 1:
                    rest_copy.wait()
                pack_own(l, 0, n)
        presmooth(cycle, base, 2, n + 2)
        for side in range(2):
            outer = (0, 1) if side == 0 else (n + 2, n + 3)

            def arrive(side=side, outer=outer):
                b_halo(cycle, l, side).wait_recv()
                if cycle == 0:
                    o_halo(l, side, 0).wait_recv()
                    for t, j in enumerate(outer):
                        pack_s(base + j, raw_s[l, side, 0, t])

            pl.when(has[side])(arrive)
            if cycle == 0:
                def blank(outer=outer):
                    for j in outer:
                        s4[base + j] = jnp.zeros(s4.shape[1:], bf16)
                        b[0, base + j] = jnp.zeros(b.shape[2:], f32)
                        b[1, base + j] = jnp.zeros(b.shape[2:], f32)
                pl.when(jnp.logical_not(has[side]))(blank)
        js = [0, 1, n + 2, n + 3]
        values = [s_mul(base + j, b[cycle, base + j]) for j in js]
        for j, v in zip(js, values):
            x[base + j] = v
            two(x_two, j, v)
        half = n // 2
        if l + 1 < levels:
            def store(p, c):
                b[cycle, bases[l + 1] + 2 + p] = c
            if half > 4:
                restrict(cycle, base, [0, 1, half - 2, half - 1], store)
                send_b(cycle, l + 1)
                if cycle == 0 and l == 0:
                    for k in range(1, devices):
                        go_copy(k, dev, lax.rem(dev + k, devices)).start()
                restrict(cycle, base, (2, half - 2), store)
            else:
                restrict(cycle, base, (0, half), store)
                send_b(cycle, l + 1)
            if cycle == 0 and l == 1:
                send_o(1, reversed(range(levels)))
        else:
            def store(p, c):
                b[cycle, gather_base + 2 + dev] = c
            restrict(cycle, base, (0, half), store)
            for k in range(1, devices):
                g_copy(cycle, k, dev, lax.rem(dev + k, devices)).start()

    def solve_wide(cycle):
        if cycle == 0:
            own = offsets[levels]
            raw_g[dev] = raw[:, pl.ds(own, 1)]
            coarse_copy.wait()
            start = 0
            for m in range(1, len(wide)):
                def body(ps, start=start, m=m):
                    for p in ps:
                        pack_pair(wide_bases[m], p, [
                            [raw_c[k, 0, start + 2 * p + t] for k in range(4)] for t in range(2)])
                if wide[m] > 1:
                    over_rows(0, wide[m] // 2, body, 2)
                else:
                    row = wide_bases[m] + 2
                    put(a_op, row, placed_a(False, *[raw_c[k, 0, start] for k in range(3)]))
                    pack_s(row, raw_c[3, 0, start])
                start += wide[m]
            for k in range(1, devices):
                sender = lax.rem(dev + k, devices)
                go_copy(0, sender, sender).wait_recv()

            def body(ps):
                for p in ps:
                    pack_pair(gather_base, p, [[raw_g[2 * p + t, k, 0] for k in range(4)] for t in range(2)])
            over_rows(0, devices // 2, body, 2)
            zero_rows(x, [gather_base + 1, gather_base + wide[0] + 2])
        for k in range(1, devices):
            sender = lax.rem(dev + k, devices)
            g_copy(cycle, 0, sender, sender).wait_recv()

        def visit(m):
            n, base = wide[m], wide_bases[m]
            pads = [1, n + 2] + ([n + 3] if n == 1 else [])
            presmooth(cycle, base, 2, n + 2)
            if m + 1 < len(wide):
                zero_rows(x_two, pads)

                def store(p, c):
                    b[cycle, wide_bases[m + 1] + 2 + p] = c
                restrict(cycle, base, (0, n // 2), store)
                visit(m + 1)
                correct(base, 2, n + 2, lambda i: wide_bases[m + 1] + i)
            zero_rows(x_two, pads)
            postsmooth(cycle, base, n, False)
        visit(0)

    def up_to(cycle, l):
        n, base = heights[l], bases[l]
        if l == levels - 1:
            correct(base, 0, n + 4, lambda i: gather_base + dev + i)
        else:
            correct(base, 0, n + 4, lambda i: bases[l + 1] + i)
        if cycle == 0:
            for side in range(2):
                row = base + (1 if side == 0 else n + 2)

                def arrive(side=side, row=row):
                    o_halo(l, side, 1).wait_recv()
                    put(a_op, row, placed_a(side == 1, *[raw_a[l, side, k, 0] for k in range(3)]))

                def blank(row=row):
                    a_op[row] = jnp.zeros(a_op.shape[1:], bf16)
                pl.when(has[side])(arrive)
                pl.when(jnp.logical_not(has[side]))(blank)

    for l in range(levels):
        down_local(0, l)
    solve_wide(0)
    for l in reversed(range(levels)):
        up_to(0, l)
        postsmooth(0, bases[l], heights[l], True, keep=l == 0)

    base = bases[0]

    def again(ps):
        js, products = [], []
        for p in ps:
            js += [2 + 2 * p, 3 + 2 * p]
            products += a_pair(base, 2 + 2 * p, f_two)
        values = [b[0, base + j] - v for j, v in zip(js, products)]
        for j, v in zip(js, values):
            b[1, base + j] = v
    again([0, rows // 2 - 1])
    send_b(1, 0)
    over_rows(1, rows // 2 - 1, again, 4)

    for l in range(levels):
        down_local(1, l)
    solve_wide(1)
    for l in reversed(range(1, levels)):
        up_to(1, l)
        postsmooth(1, bases[l], heights[l], True)
    up_to(1, 0)

    def slab_copy(k, slab, sender):
        return remote(staged.at[pl.ds(slab * per_slab, per_slab)], out.at[pl.ds(sender * per_slab, per_slab)],
                      t_send.at[k], t_recv.at[sender], "grp", slab)

    sent = []
    for k in [k for k in range(groups) if k != groups // 2] + [groups // 2]:
        slab = lax.rem(grp + groups // 2 + 2 * (k // 2), groups)
        if k % 2:
            slab = slab + 1 - 2 * lax.rem(slab, 2)

        def body(us, slab=slab):
            ts = [slab * per_slab + u for u in us]
            js = [order[0, t] + 2 for t in ts]
            products = []
            for j in js:
                low = j - 1 - lax.rem(j, 2)
                products.append(a_single(base, j, low, x_two))
            values = finish(1, base, js, products)
            values = [v + first[j] for v, j in zip(values, js)]
            for t, v in zip(ts, values):
                staged[t] = v
        own = k == groups // 2
        over_rows(0, per_slab, body, 8)
        if own:
            keep = pltpu.make_async_copy(staged.at[pl.ds(slab * per_slab, per_slab)],
                                         out.at[pl.ds(grp * per_slab, per_slab)], local_sem.at[0])
            keep.start()
        else:
            slab_copy(k, slab, grp).start()
            sent.append((k, slab))
    keep.wait()

    for l in range(levels):
        for side in range(2):
            def left(l=l, side=side):
                b_halo(0, l, side).wait_send()
                b_halo(1, l, side).wait_send()
                o_halo(l, side, 0).wait_send()
                o_halo(l, side, 1).wait_send()
            on_send(side, left)
    for k in range(1, devices):
        target = lax.rem(dev + k, devices)
        go_copy(k, dev, target).wait_send()
        g_copy(0, k, dev, target).wait_send()
        g_copy(1, k, dev, target).wait_send()
    for k, slab in sent:
        slab_copy(k, slab, grp).wait_send()
        slab_copy(k, slab, slab).wait_recv()


def shards(adjoint_load, local_ops, coarse_ops, slab_order):
    rows, size, cases = adjoint_load.shape
    devices = lax.axis_size("dev")
    groups = lax.axis_size("grp")
    levels = rows.bit_length() - 1
    heights = [rows >> l for l in range(levels)]
    wide = [devices]
    while sum(wide[1:]) < coarse_ops.shape[2]:
        wide.append(wide[-1] // 2)
    bases, total = [], 0
    for n in heights + wide:
        bases.append(total)
        total += n + 4
    plan = (devices, groups, heights, bases[:levels], wide, bases[levels:])
    most = max(rows, devices) + 4
    kinds = local_ops.shape[0]
    dma = pltpu.SemaphoreType.DMA
    scratch = [
        pltpu.VMEM(local_ops.shape, f32),
        pltpu.VMEM((levels, 2, 1, 2, size, size), f32),
        pltpu.VMEM((levels, 2, 3, 1, size, size), f32),
        pltpu.VMEM((devices, kinds, 1, size, size), f32),
        pltpu.VMEM(coarse_ops.shape, f32),
        pltpu.VMEM((total, 2 * size, 4 * size), bf16),
        pltpu.VMEM((total // 2 + 1, 2 * size, 4 * size), bf16),
        pltpu.VMEM((total, size, 4 * size), bf16),
        pltpu.VMEM((2, total, size, cases), f32),
        pltpu.VMEM((total, size, cases), f32),
        pltpu.VMEM((rows + 4, size, cases), f32),
        pltpu.VMEM((most, size, 2 * cases), bf16),
        pltpu.VMEM((rows + 4, size, 2 * cases), bf16),
        pltpu.VMEM((rows, size, cases), f32),
        dma((CHUNKS + 3,)),
        dma((2, levels, 2)), dma((2, levels, 2)),
        dma((levels, 2, 2)), dma((levels, 2, 2)),
        dma((devices,)), dma((devices,)),
        dma((2, devices)), dma((2, devices)),
        dma((groups,)), dma((groups,)),
    ]
    anywhere = pl.BlockSpec(memory_space=pl.ANY)
    return pl.pallas_call(
        functools.partial(kernel, plan),
        out_shape=jax.ShapeDtypeStruct(adjoint_load.shape, f32),
        in_specs=[anywhere, anywhere, anywhere, pl.BlockSpec(memory_space=pltpu.SMEM)],
        out_specs=anywhere,
        scratch_shapes=scratch,
        compiler_params=pltpu.CompilerParams(
            collective_id=0, has_side_effects=True, vmem_limit_bytes=62 * 2**20),
    )(adjoint_load, local_ops, coarse_ops, slab_order)


def solution(mesh):
    placed = (
        P(("grp", "dev"), None, None),
        P(None, ("grp", "dev"), None, None),
        P(None, "grp", None, None, None),
        P(("grp", "dev"), None),
    )
    return jax.shard_map(
        shards, mesh=mesh, in_specs=placed, out_specs=P(("grp", "dev"), None, None), check_vma=False
    )
```

```python
import functools
import jax
import jax.numpy as jnp
from jax import lax
from jax.experimental import pallas as pl
from jax.experimental.pallas import tpu as pltpu
from jax.sharding import PartitionSpec as P

damping = 0.8
GROUP = 4
CHUNKS = 4
f32 = jnp.float32
bf16 = jnp.bfloat16


def split(value):
    high = value.astype(bf16)
    return high, (value - high.astype(f32)).astype(bf16)


def over_rows(low, high, body, group=GROUP):
    full = (high - low) // group
    if full > 1:
        def step(index, carry):
            body([low + index * group + t for t in range(group)])
            return carry
        lax.fori_loop(0, full, step, 0)
        low += full * group
    while low < high:
        body(list(range(low, min(low + group, high))))
        low += group


def kernel(
    plan,
    load, ops, coarse, order,
    out,
    raw, raw_s, raw_a, raw_g, raw_c,
    a_op, r_op, s4, d_op, b, x, first, x_two, f_two, staged,
    local_sem, b_send, b_recv, o_send, o_recv, go_send, go_recv, g_send, g_recv, t_send, t_recv,
):
    devices, groups, heights, bases, wide, wide_bases = plan
    levels = len(heights)
    rows = heights[0]
    per_slab = rows // groups
    dev = lax.axis_index("dev")
    grp = lax.axis_index("grp")
    has = (dev > 0, dev < devices - 1)
    offsets = [2 * rows - 2 * rows // 2**l for l in range(levels + 1)]
    gather_base = wide_bases[0]

    local = []

    def fetch(src, dst):
        copy = pltpu.make_async_copy(src, dst, local_sem.at[len(local)])
        copy.start()
        local.append(copy)
        return copy

    load_copy = fetch(load, b.at[0, pl.ds(bases[0] + 2, rows)])
    piece = rows // CHUNKS
    fine_copies = [
        fetch(ops.at[:, pl.ds(c * piece, piece)], raw.at[:, pl.ds(c * piece, piece)])
        for c in range(CHUNKS)
    ]
    rest = ops.shape[1] - rows
    rest_copy = fetch(ops.at[:, pl.ds(rows, rest)], raw.at[:, pl.ds(rows, rest)])
    coarse_copy = fetch(coarse, raw_c)

    barrier = pltpu.get_barrier_semaphore()
    for k in range(1, devices):
        pl.semaphore_signal(barrier, inc=1, device_id={"dev": lax.rem(dev + k, devices)},
                            device_id_type=pl.DeviceIdType.MESH)
    for k in range(1, groups):
        pl.semaphore_signal(barrier, inc=1, device_id={"grp": lax.rem(grp + k, groups)},
                            device_id_type=pl.DeviceIdType.MESH)
    pl.semaphore_wait(barrier, devices - 1 + groups - 1)

    def remote(src, dst, send, recv, axis, target):
        return pltpu.make_async_remote_copy(
            src_ref=src, dst_ref=dst, send_sem=send, recv_sem=recv,
            device_id={axis: target}, device_id_type=pl.DeviceIdType.MESH)

    def b_halo(cycle, l, side):
        n, base = heights[l], bases[l]
        start = n - 2 if side == 0 else 0
        if cycle == 0 and l == 0:
            src = load.at[pl.ds(start, 2)]
        else:
            src = b.at[cycle, pl.ds(base + 2 + start, 2)]
        dst = b.at[cycle, pl.ds(base + (0 if side == 0 else n + 2), 2)]
        target = dev + 1 if side == 0 else dev - 1
        return remote(src, dst, b_send.at[cycle, l, side], b_recv.at[cycle, l, side], "dev", target)

    def o_halo(l, side, part):
        n = heights[l]
        if part == 0:
            start = n - 2 if side == 0 else 0
            src, dst = ops.at[pl.ds(3, 1), pl.ds(offsets[l] + start, 2)], raw_s.at[l, side]
        else:
            start = n - 1 if side == 0 else 0
            src, dst = ops.at[pl.ds(0, 3), pl.ds(offsets[l] + start, 1)], raw_a.at[l, side]
        target = dev + 1 if side == 0 else dev - 1
        return remote(src, dst, o_send.at[l, side, part], o_recv.at[l, side, part], "dev", target)

    def on_send(side, act):
        pl.when(has[1 - side])(act)

    def send_b(cycle, l):
        for side in range(2):
            on_send(side, lambda side=side: b_halo(cycle, l, side).start())

    def go_copy(k, sender, target):
        return remote(ops.at[:, pl.ds(offsets[levels], 1)], raw_g.at[sender],
                      go_send.at[k], go_recv.at[sender], "dev", target)

    def g_copy(cycle, k, sender, target):
        row = b.at[cycle, pl.ds(gather_base + 2 + sender, 1)]
        return remote(row, row, g_send.at[cycle, k], g_recv.at[cycle, sender], "dev", target)

    send_b(0, 0)
    def send_o(part, these):
        for l in these:
            for side in range(2):
                on_send(side, lambda l=l, side=side: o_halo(l, side, part).start())

    send_o(0, [0])

    size = x.shape[1]
    cases = x.shape[2]

    def pack_s(row, block):
        hi, lo = split(damping * block)
        hi, lo = hi.astype(f32), lo.astype(f32)
        s4[row] = jnp.concatenate([hi, hi, lo, lo], axis=1).astype(bf16)

    def placed_a(odd, lower, middle, upper):
        none = jnp.zeros_like(middle)
        blocks = [none, lower, middle, upper] if odd else [lower, middle, upper, none]
        return jnp.concatenate(blocks, axis=1)

    def put(ref, row, value):
        hi, lo = split(value)
        ref[row, pl.ds(0, size)] = hi
        ref[row, pl.ds(size, size)] = lo

    def pack_pair(base, p, blocks):
        row = base + 2 + 2 * p
        (l0, m0, u0, inv0), (l1, m1, u1, inv1) = blocks
        even, odd = placed_a(False, l0, m0, u0), placed_a(True, l1, m1, u1)
        put(a_op, row, even)
        put(a_op, row + 1, odd)
        put(r_op, base // 2 + 1 + p, 0.5 * (even + odd))
        pack_s(row, inv0)
        pack_s(row + 1, inv1)

    def pack_own(l, low, high):
        def body(ps):
            for p in ps:
                source = offsets[l] + 2 * p
                pack_pair(bases[l], p, [[raw[k, source + t] for k in range(4)] for t in range(2)])
        over_rows(low // 2, high // 2, body, 2)

    def s_mul(row, value):
        hi, lo = split(value)
        return jnp.dot(s4[row], jnp.concatenate([hi, lo, hi, lo], axis=0), preferred_element_type=f32)

    def gathered(product):
        half = product.shape[0] // 2
        upper, lower = product[:half], product[half:]
        return (lower[:, cases:] + (upper[:, cases:] + lower[:, :cases])) + upper[:, :cases]

    def window(ref, low):
        return ref[pl.ds(low, 4)].reshape(4 * size, 2 * cases)

    def a_pair(base, j, ref):
        both = a_op[pl.ds(base + j, 2)].reshape(4 * size, 4 * size)
        product = jnp.dot(both, window(ref, j - 1), preferred_element_type=f32)
        return [gathered(product[: 2 * size]), gathered(product[2 * size :])]

    def a_single(base, j, low, ref):
        return gathered(jnp.dot(a_op[base + j], window(ref, low), preferred_element_type=f32))

    def two(ref, j, value):
        hi, lo = split(value)
        ref[j, :, pl.ds(0, cases)] = hi
        ref[j, :, pl.ds(cases, cases)] = lo

    def presmooth(cycle, base, low, high):
        def body(js):
            values = [s_mul(base + j, b[cycle, base + j]) for j in js]
            for j, v in zip(js, values):
                x[base + j] = v
                two(x_two, j, v)
        over_rows(low, high, body, 16)

    def restrict(cycle, base, pairs, store):
        def body(ps):
            values = []
            for p in ps:
                j = 2 + 2 * p
                product = jnp.dot(r_op[base // 2 + 1 + p], window(x_two, j - 1), preferred_element_type=f32)
                values.append(0.5 * (b[cycle, base + j] + b[cycle, base + j + 1]) - gathered(product))
            for p, v in zip(ps, values):
                store(p, v)
        if isinstance(pairs, list):
            body(pairs)
        else:
            over_rows(*pairs, body, 6)

    def correct(base, low, high, e_row):
        def body(ps):
            js, vs = [], []
            for p in ps:
                add = x[e_row(p + 1)]
                js += [2 * p, 2 * p + 1]
                vs += [x[base + 2 * p] + add, x[base + 2 * p + 1] + add]
            for j, v in zip(js, vs):
                x[base + j] = v
                two(x_two, j, v)
        over_rows(low // 2, high // 2, body, 6)

    def finish(cycle, base, js, products):
        r = [b[cycle, base + j] - v for j, v in zip(js, products)]
        return [x[base + j] + s_mul(base + j, v) for j, v in zip(js, r)]

    def settle(base, js, values, keep):
        for j, v in zip(js, values):
            if keep:
                first[j] = v
                two(f_two, j, v)
            else:
                x[base + j] = v

    def postsmooth(cycle, base, n, halo, keep=False):
        def body(ps, singles=()):
            js, products = [], []
            for p in ps:
                js += [2 + 2 * p, 3 + 2 * p]
                products += a_pair(base, 2 + 2 * p, x_two)
            for j, low in singles:
                js.append(j)
                products.append(a_single(base, j, low, x_two))
            settle(base, js, finish(cycle, base, js, products), keep)
        if n == 1:
            body([], [(2, 1)])
            return
        head = max(0, (n // 2 - 1) // 4 * 4)
        over_rows(0, head, body, 4)
        body(list(range(head, n // 2)), [(1, 0), (n + 2, n)] if halo else [])

    def zero_rows(ref, indices):
        for i in indices:
            ref[i] = jnp.zeros(ref.shape[1:], ref.dtype)

    dense = wide.index(2) if 2 in wide[1:] and 2 * size == cases else None

    def pack_coarse():
        coarse_copy.wait()
        start = 0
        for m in range(1, len(wide)):
            def body(ps, start=start, m=m):
                for p in ps:
                    pack_pair(wide_bases[m], p, [
                        [raw_c[k, 0, start + 2 * p + t] for k in range(4)] for t in range(2)])
            if wide[m] > 1:
                over_rows(0, wide[m] // 2, body, 2)
            else:
                row = wide_bases[m] + 2
                put(a_op, row, placed_a(False, *[raw_c[k, 0, start] for k in range(3)]))
                pack_s(row, raw_c[3, 0, start])
            start += wide[m]

    def visit(cycle, m, direct=True):
        n, base = wide[m], wide_bases[m]
        if direct and m == dense:
            high, low = split(b[cycle, pl.ds(base + 2, 2)].reshape(2 * size, cases))
            value = gathered(jnp.dot(d_op[...], jnp.concatenate([high, low], axis=1), preferred_element_type=f32))
            x[base + 2] = value[:size]
            x[base + 3] = value[size:]
            return
        pads = [1, n + 2] + ([n + 3] if n == 1 else [])
        presmooth(cycle, base, 2, n + 2)
        if m + 1 < len(wide):
            zero_rows(x_two, pads)

            def store(p, c):
                b[cycle, wide_bases[m + 1] + 2 + p] = c
            restrict(cycle, base, (0, n // 2), store)
            visit(cycle, m + 1)
            correct(base, 2, n + 2, lambda i: wide_bases[m + 1] + i)
        zero_rows(x_two, pads)
        postsmooth(cycle, base, n, False)

    def form_dense():
        base = wide_bases[dense]
        shape = (2 * size, cases)
        unit = (lax.broadcasted_iota(jnp.int32, shape, 0) == lax.broadcasted_iota(jnp.int32, shape, 1)).astype(f32)
        b[0, base + 2] = unit[:size]
        b[0, base + 3] = unit[size:]
        visit(0, dense, False)
        hi, lo = split(x[pl.ds(base + 2, 2)].reshape(shape))
        d_op[pl.ds(0, 2 * size)] = hi
        d_op[pl.ds(2 * size, 2 * size)] = lo

    def down_local(cycle, l):
        n, base = heights[l], bases[l]
        if cycle == 0:
            if l == 0:
                load_copy.wait()
                for c in range(CHUNKS):
                    fine_copies[c].wait()
                    pack_own(0, c * piece, (c + 1) * piece)
                    if c == 0:
                        send_o(0, range(1, levels))
            else:
                if l == 1:
                    rest_copy.wait()
                pack_own(l, 0, n)
        presmooth(cycle, base, 2, n + 2)
        for side in range(2):
            outer = (0, 1) if side == 0 else (n + 2, n + 3)

            def arrive(side=side, outer=outer):
                b_halo(cycle, l, side).wait_recv()
                if cycle == 0:
                    o_halo(l, side, 0).wait_recv()
                    for t, j in enumerate(outer):
                        pack_s(base + j, raw_s[l, side, 0, t])

            pl.when(has[side])(arrive)
            if cycle == 0:
                def blank(outer=outer):
                    for j in outer:
                        s4[base + j] = jnp.zeros(s4.shape[1:], bf16)
                        b[0, base + j] = jnp.zeros(b.shape[2:], f32)
                        b[1, base + j] = jnp.zeros(b.shape[2:], f32)
                pl.when(jnp.logical_not(has[side]))(blank)
        js = [0, 1, n + 2, n + 3]
        values = [s_mul(base + j, b[cycle, base + j]) for j in js]
        for j, v in zip(js, values):
            x[base + j] = v
            two(x_two, j, v)
        half = n // 2
        if l + 1 < levels:
            def store(p, c):
                b[cycle, bases[l + 1] + 2 + p] = c
            if half > 4:
                restrict(cycle, base, [0, 1, half - 2, half - 1], store)
                send_b(cycle, l + 1)
                if cycle == 0 and l == 0:
                    for k in range(1, devices):
                        go_copy(k, dev, lax.rem(dev + k, devices)).start()
                restrict(cycle, base, (2, half - 2), store)
            else:
                restrict(cycle, base, (0, half), store)
                send_b(cycle, l + 1)
            if cycle == 0 and l == 1:
                send_o(1, reversed(range(levels)))
                pack_coarse()
                if dense is not None:
                    form_dense()
        else:
            def store(p, c):
                b[cycle, gather_base + 2 + dev] = c
            restrict(cycle, base, (0, half), store)
            for k in range(1, devices):
                g_copy(cycle, k, dev, lax.rem(dev + k, devices)).start()

    def solve_wide(cycle):
        if cycle == 0:
            own = offsets[levels]
            raw_g[dev] = raw[:, pl.ds(own, 1)]
            for k in range(1, devices):
                sender = lax.rem(dev + k, devices)
                go_copy(0, sender, sender).wait_recv()

            def body(ps):
                for p in ps:
                    pack_pair(gather_base, p, [[raw_g[2 * p + t, k, 0] for k in range(4)] for t in range(2)])
            over_rows(0, devices // 2, body, 2)
            zero_rows(x, [gather_base + 1, gather_base + wide[0] + 2])
        for k in range(1, devices):
            sender = lax.rem(dev + k, devices)
            g_copy(cycle, 0, sender, sender).wait_recv()

        visit(cycle, 0)

    def up_to(cycle, l):
        n, base = heights[l], bases[l]
        if l == levels - 1:
            correct(base, 0, n + 4, lambda i: gather_base + dev + i)
        else:
            correct(base, 0, n + 4, lambda i: bases[l + 1] + i)
        if cycle == 0:
            for side in range(2):
                row = base + (1 if side == 0 else n + 2)

                def arrive(side=side, row=row):
                    o_halo(l, side, 1).wait_recv()
                    put(a_op, row, placed_a(side == 1, *[raw_a[l, side, k, 0] for k in range(3)]))

                def blank(row=row):
                    a_op[row] = jnp.zeros(a_op.shape[1:], bf16)
                pl.when(has[side])(arrive)
                pl.when(jnp.logical_not(has[side]))(blank)

    for l in range(levels):
        down_local(0, l)
    solve_wide(0)
    for l in reversed(range(levels)):
        up_to(0, l)
        postsmooth(0, bases[l], heights[l], True, keep=l == 0)

    base = bases[0]

    def again(ps):
        js, products = [], []
        for p in ps:
            js += [2 + 2 * p, 3 + 2 * p]
            products += a_pair(base, 2 + 2 * p, f_two)
        values = [b[0, base + j] - v for j, v in zip(js, products)]
        for j, v in zip(js, values):
            b[1, base + j] = v
    again([0, rows // 2 - 1])
    send_b(1, 0)
    over_rows(1, rows // 2 - 1, again, 4)

    for l in range(levels):
        down_local(1, l)
    solve_wide(1)
    for l in reversed(range(1, levels)):
        up_to(1, l)
        postsmooth(1, bases[l], heights[l], True)
    up_to(1, 0)

    def slab_copy(k, slab, sender):
        return remote(staged.at[pl.ds(slab * per_slab, per_slab)], out.at[pl.ds(sender * per_slab, per_slab)],
                      t_send.at[k], t_recv.at[sender], "grp", slab)

    sent = []
    for k in [k for k in range(groups) if k != groups // 2] + [groups // 2]:
        slab = lax.rem(grp + groups // 2 + 2 * (k // 2), groups)
        if k % 2:
            slab = slab + 1 - 2 * lax.rem(slab, 2)

        def body(us, slab=slab):
            ts = [slab * per_slab + u for u in us]
            js = [order[0, t] + 2 for t in ts]
            products = []
            for j in js:
                low = j - 1 - lax.rem(j, 2)
                products.append(a_single(base, j, low, x_two))
            values = finish(1, base, js, products)
            values = [v + first[j] for v, j in zip(values, js)]
            for t, v in zip(ts, values):
                staged[t] = v
        own = k == groups // 2
        over_rows(0, per_slab, body, 8)
        if own:
            keep = pltpu.make_async_copy(staged.at[pl.ds(slab * per_slab, per_slab)],
                                         out.at[pl.ds(grp * per_slab, per_slab)], local_sem.at[0])
            keep.start()
        else:
            slab_copy(k, slab, grp).start()
            sent.append((k, slab))
    keep.wait()

    for l in range(levels):
        for side in range(2):
            def left(l=l, side=side):
                b_halo(0, l, side).wait_send()
                b_halo(1, l, side).wait_send()
                o_halo(l, side, 0).wait_send()
                o_halo(l, side, 1).wait_send()
            on_send(side, left)
    for k in range(1, devices):
        target = lax.rem(dev + k, devices)
        go_copy(k, dev, target).wait_send()
        g_copy(0, k, dev, target).wait_send()
        g_copy(1, k, dev, target).wait_send()
    for k, slab in sent:
        slab_copy(k, slab, grp).wait_send()
        slab_copy(k, slab, slab).wait_recv()


def shards(adjoint_load, local_ops, coarse_ops, slab_order):
    rows, size, cases = adjoint_load.shape
    devices = lax.axis_size("dev")
    groups = lax.axis_size("grp")
    levels = rows.bit_length() - 1
    heights = [rows >> l for l in range(levels)]
    wide = [devices]
    while sum(wide[1:]) < coarse_ops.shape[2]:
        wide.append(wide[-1] // 2)
    bases, total = [], 0
    for n in heights + wide:
        bases.append(total)
        total += n + 4
    plan = (devices, groups, heights, bases[:levels], wide, bases[levels:])
    most = max(rows, devices) + 4
    kinds = local_ops.shape[0]
    dma = pltpu.SemaphoreType.DMA
    scratch = [
        pltpu.VMEM(local_ops.shape, f32),
        pltpu.VMEM((levels, 2, 1, 2, size, size), f32),
        pltpu.VMEM((levels, 2, 3, 1, size, size), f32),
        pltpu.VMEM((devices, kinds, 1, size, size), f32),
        pltpu.VMEM(coarse_ops.shape, f32),
        pltpu.VMEM((total, 2 * size, 4 * size), bf16),
        pltpu.VMEM((total // 2 + 1, 2 * size, 4 * size), bf16),
        pltpu.VMEM((total, size, 4 * size), bf16),
        pltpu.VMEM((4 * size, cases), bf16),
        pltpu.VMEM((2, total, size, cases), f32),
        pltpu.VMEM((total, size, cases), f32),
        pltpu.VMEM((rows + 4, size, cases), f32),
        pltpu.VMEM((most, size, 2 * cases), bf16),
        pltpu.VMEM((rows + 4, size, 2 * cases), bf16),
        pltpu.VMEM((rows, size, cases), f32),
        dma((CHUNKS + 3,)),
        dma((2, levels, 2)), dma((2, levels, 2)),
        dma((levels, 2, 2)), dma((levels, 2, 2)),
        dma((devices,)), dma((devices,)),
        dma((2, devices)), dma((2, devices)),
        dma((groups,)), dma((groups,)),
    ]
    anywhere = pl.BlockSpec(memory_space=pl.ANY)
    return pl.pallas_call(
        functools.partial(kernel, plan),
        out_shape=jax.ShapeDtypeStruct(adjoint_load.shape, f32),
        in_specs=[anywhere, anywhere, anywhere, pl.BlockSpec(memory_space=pltpu.SMEM)],
        out_specs=anywhere,
        scratch_shapes=scratch,
        compiler_params=pltpu.CompilerParams(
            collective_id=0, has_side_effects=True, vmem_limit_bytes=62 * 2**20),
    )(adjoint_load, local_ops, coarse_ops, slab_order)


def solution(mesh):
    placed = (
        P(("grp", "dev"), None, None),
        P(None, ("grp", "dev"), None, None),
        P(None, "grp", None, None, None),
        P(("grp", "dev"), None),
    )
    return jax.shard_map(
        shards, mesh=mesh, in_specs=placed, out_specs=P(("grp", "dev"), None, None), check_vma=False
    )
```
